512 devices in a mesh: tx: 16 (over z), ty: 32 (over y, x, core).
Axes of the slice: x: 4, y: 4, z: 16, core: 2. Of those that a mesh axis runs over, the one named last changes fastest.
Arguments:
- embedding: float32 [50, 16, 32, 512], P(None, 'tx', 'ty'), may hold values from -8 to 8
- neighbors: int32 [15, 16, 32, 512], P(None, 'tx', 'ty'), may hold values from 0 to 1663, as said below
- slide_id: int32 [16, 32, 512], P('tx', 'ty'), may hold values from 0 to 39, as said below
- live_count: int32 [16, 32], P('tx', 'ty'), may hold values from 128 to 512, as said below
- centroids: float32 [100, 50], replicated, may hold values from -6 to 6
Outputs:
- corrected: float32 [50, 16, 32, 512], P(None, 'tx', 'ty')
- centers: float32 [100, 50], replicated
The draws below stay inside these ranges and needn't reach their ends.
Inputs may be any that keep to these rules, and one draw needn't show every extreme that they name: `neighbors`: each id names a live cell, either of the cell's own tile or of one of the up to eight bordering tiles inside the grid; an id in a bordering tile names one of that tile's first 128 cells. `slide_id`: the cell slots of one tile, live or not, carry at most 4 distinct slides. The live cells of a tile are its first live_count slots; some tile is full in every draw.
All inputs are finite; a program needn't handle non-finite values.
Results may differ from the reference program's by a relative error of at most 0.0003.
Values sent between devices are 32-bit elements; how exact they have to be, the bound alone decides.
A program may use at most 64 MiB of HBM per device.

```python
import jax
import jax.numpy as jnp
from jax import lax

PCS = 50
CLUSTERS = 100
SLIDES = 40
NEIGHBORS = 15
SLOTS = 4
ITERS = 2
CELLS_DEV = 512
BOUND = 128
TILES_X = 16
TILES_Y = 32


def live_table(key):
    key = jax.random.fold_in(key, 11)
    tiles = TILES_X * TILES_Y
    order = lax.broadcasted_iota(jnp.int32, (TILES_X, TILES_Y), 0) * TILES_Y + lax.broadcasted_iota(jnp.int32, (TILES_X, TILES_Y), 1)
    span = (CELLS_DEV - BOUND) * (tiles - 1 - order) // tiles
    cut = jax.random.randint(key, (TILES_X, TILES_Y), 0, 1 << 30) % (span + 1)
    return (CELLS_DEV - cut).astype(jnp.int32)


def slide_choice(key):
    key = jax.random.fold_in(key, 23)
    first_key, second_key = jax.random.split(key)
    ident = lax.broadcasted_iota(jnp.int32, (TILES_X, TILES_Y, SLIDES), 2)
    scores = jax.random.randint(first_key, (TILES_X, TILES_Y, SLIDES), 0, 1 << 20) * SLIDES + ident
    _, table = lax.top_k(scores, SLOTS)
    slot = jax.random.randint(second_key, (TILES_X, TILES_Y, CELLS_DEV), 0, SLOTS)
    return jnp.take_along_axis(table.astype(jnp.int32), slot, axis=2).astype(jnp.int32)


def draw_live_count(key, part):
    return live_table(key)


def draw_slide_id(key, part):
    key = jax.random.fold_in(key, 5)
    return slide_choice(key)


def draw_embedding(key, part):
    slides = slide_choice(jax.random.fold_in(key, 5))
    key = jax.random.fold_in(key, 41)
    noise_key, offset_key = jax.random.split(key)
    shape = (PCS, TILES_X, TILES_Y, CELLS_DEV)
    noise = jax.random.normal(noise_key, shape, jnp.float32)
    offsets = jax.random.normal(offset_key, (PCS, SLIDES), jnp.float32)
    shifted = jnp.take(offsets, slides, axis=1)
    return jnp.clip(noise + shifted, -8.0, 8.0).astype(jnp.float32)


def draw_neighbors(key, part):
    alive = live_table(key)
    key = jax.random.fold_in(key, 31)
    keys = jax.random.split(key, 4)
    shape = (NEIGHBORS, TILES_X, TILES_Y, CELLS_DEV)
    row = lax.broadcasted_iota(jnp.int32, shape, 1)
    col = lax.broadcasted_iota(jnp.int32, shape, 2)
    far = jax.random.randint(keys[0], shape, 0, 10) < 3
    step_x = jnp.where(far, jax.random.randint(keys[1], shape, -1, 2), 0)
    step_y = jnp.where(far, jax.random.randint(keys[2], shape, -1, 2), 0)
    dest_x = jnp.clip(row + step_x, 0, TILES_X - 1)
    dest_y = jnp.clip(col + step_y, 0, TILES_Y - 1)
    moved = (dest_x != row) | (dest_y != col)
    direction = (dest_x - row + 1) * 3 + (dest_y - col + 1)
    drawn = jax.random.randint(keys[3], shape, 0, 1 << 30)
    outer = CELLS_DEV + direction * BOUND + drawn % BOUND
    inner = drawn % alive[None, :, :, None]
    return jnp.where(moved, outer, inner).astype(jnp.int32)


def bell_draw(rng, dims, deviation, bound, held_as=jnp.bfloat16):
    return jnp.clip(deviation * jax.random.normal(rng, dims, jnp.float32), -bound, bound).astype(held_as)


def setup_inputs(seed: int = 0) -> dict:
    splits = jax.random.split(jax.random.key(seed), 6)
    return {
        "embedding": draw_embedding(jax.random.fold_in(splits[5], 71), 0),
        "neighbors": draw_neighbors(jax.random.fold_in(splits[5], 71), 0),
        "slide_id": draw_slide_id(jax.random.fold_in(splits[5], 71), 0),
        "live_count": draw_live_count(jax.random.fold_in(splits[5], 71), 0),
        "centroids": bell_draw(splits[4], (CLUSTERS, PCS), 1.0, 6.0, jnp.float32),
    }


HIGH = lax.Precision.HIGHEST
SHARPNESS = 20.0

def unit_columns(values):
    return values / jnp.sqrt(lax.optimization_barrier(jnp.sum(values * values, axis=0, keepdims=True)) + 1.0)

def unit_rows(values):
    return values / jnp.sqrt(lax.optimization_barrier(jnp.sum(values * values, axis=1, keepdims=True)) + 1.0)

def layout(slides, alive):
    cells = slides.shape[0]
    ident = lax.broadcasted_iota(jnp.int32, (SLIDES, cells), 0)
    same = slides[None, :] == ident
    member = same & alive[None, :]
    present = jnp.any(member, axis=1).astype(jnp.int32)
    rank = (jnp.cumsum(present) - present).astype(jnp.int32)
    cell_rank = lax.optimization_barrier(jnp.sum(jnp.where(same, rank[:, None], 0), axis=0)).astype(jnp.int32)
    slot_ids = lax.broadcasted_iota(jnp.int32, (SLOTS, 1), 0)
    livef = alive.astype(jnp.float32)
    masks = (cell_rank[None, :] == slot_ids).astype(jnp.float32) * livef[None, :]
    place = ((rank[None, :] == slot_ids) & (present[None, :] > 0)).astype(jnp.float32)
    return (same.astype(jnp.float32), member.astype(jnp.float32), masks, place, livef)

def affinity(unit_y, values):
    unit_z = unit_columns(values)
    score = jnp.dot(unit_y, unit_z, precision=HIGH)
    return (jnp.exp(SHARPNESS * (score - 1.0)), unit_z)

def global_ids(neighbors):
    shape = neighbors.shape
    row = lax.broadcasted_iota(jnp.int32, shape, 1)
    col = lax.broadcasted_iota(jnp.int32, shape, 2)
    outer = neighbors >= CELLS_DEV
    rel = jnp.maximum(neighbors - CELLS_DEV, 0).astype(jnp.int32)
    direction = (rel // BOUND).astype(jnp.int32)
    spot = (rel % BOUND).astype(jnp.int32)
    dest_x = (row + direction // 3 - 1).astype(jnp.int32)
    dest_y = (col + direction % 3 - 1).astype(jnp.int32)
    far_id = (dest_x * TILES_Y + dest_y) * CELLS_DEV + spot
    near_id = (row * TILES_Y + col) * CELLS_DEV + neighbors
    return jnp.where(outer, far_id, near_id).astype(jnp.int32)

def reference(embedding, neighbors, slide_id, live_count, centroids):
    tiles = TILES_X * TILES_Y
    flat = embedding.reshape(PCS, tiles * CELLS_DEV)
    ids = global_ids(neighbors).reshape(NEIGHBORS, tiles * CELLS_DEV)
    total = flat
    for step in range(NEIGHBORS):
        total = total + jnp.take(flat, ids[step], axis=1)
    alive = (lax.broadcasted_iota(jnp.int32, (TILES_X, TILES_Y, CELLS_DEV), 2) < live_count[:, :, None]).reshape(tiles, CELLS_DEV)
    slides = slide_id.reshape(tiles, CELLS_DEV)
    smooth = (total / (NEIGHBORS + 1.0)).reshape(PCS, tiles, CELLS_DEV).transpose(1, 0, 2)
    smooth = smooth * alive.astype(jnp.float32)[:, None, :]
    ident = lax.broadcasted_iota(jnp.int32, (SLIDES, tiles * CELLS_DEV), 0)
    member_all = (slides.reshape(-1)[None, :] == ident) & alive.reshape(-1)[None, :]
    slide_totals = lax.optimization_barrier(jnp.sum(member_all.astype(jnp.float32), axis=1))
    field = smooth
    centre = centroids
    for turn in range(ITERS):
        unit_y = unit_rows(centre)

        def first_tile(carry, item):
            tile_z, tile_s, tile_l = item
            same, member, masks, place, livef = layout(tile_s, tile_l)
            raw, unit_z = affinity(unit_y, tile_z)
            first = raw / lax.optimization_barrier(jnp.sum(raw, axis=0, keepdims=True)) * livef[None, :]
            return (carry + jnp.dot(first, member.T, precision=HIGH), None)
        occupied, _ = lax.scan(first_tile, jnp.zeros((CLUSTERS, SLIDES), jnp.float32), (field, slides, alive))
        expected = lax.optimization_barrier(jnp.sum(occupied, axis=1, keepdims=True)) * slide_totals[None, :] / jnp.sum(slide_totals)
        ratio = ((expected + 1.0) / (occupied + 1.0)) ** 2

        def assign_tile(tile_z, tile_s, tile_l):
            same, member, masks, place, livef = layout(tile_s, tile_l)
            raw, unit_z = affinity(unit_y, tile_z)
            weighted = raw * jnp.dot(ratio, same, precision=HIGH)
            assign = weighted / lax.optimization_barrier(jnp.sum(weighted, axis=0, keepdims=True)) * livef[None, :]
            return (assign, unit_z, member, masks, place)

        def stat_tile(carry, item):
            tile_z = item[0]
            assign, unit_z, member, masks, place = assign_tile(*item)
            slot_sums = jnp.stack([jnp.dot(assign * masks[slot][None, :], tile_z.T, precision=HIGH) for slot in range(SLOTS)])
            counts = carry[0] + jnp.dot(assign, member.T, precision=HIGH)
            sums = carry[1] + jnp.einsum('sb,skd->kbd', place, slot_sums, precision=HIGH)
            centres = carry[2] + jnp.dot(assign, unit_z.T, precision=HIGH)
            return ((counts, sums, centres), None)
        start = (jnp.zeros((CLUSTERS, SLIDES), jnp.float32), jnp.zeros((CLUSTERS, SLIDES, PCS), jnp.float32), jnp.zeros((CLUSTERS, PCS), jnp.float32))
        (counts, sums, centre_sums), _ = lax.scan(stat_tile, start, (field, slides, alive))
        scale = 1.0 / (counts + 1.0)
        mean = lax.optimization_barrier(jnp.sum(sums * scale[:, :, None], axis=1)) / lax.optimization_barrier(jnp.sum(counts * scale, axis=1))[:, None]
        beta = (sums - counts[:, :, None] * mean[:, None, :]) * scale[:, :, None]

        def correct_tile(item):
            tile_z = item[0]
            assign, unit_z, member, masks, place = assign_tile(*item)
            slot_beta = jnp.einsum('sb,kbd->skd', place, beta, precision=HIGH)
            shift = jnp.zeros_like(tile_z)
            for slot in range(SLOTS):
                shift = shift + jnp.dot(slot_beta[slot].T, assign, precision=HIGH) * masks[slot][None, :]
            return tile_z - shift
        field = lax.map(correct_tile, (field, slides, alive))
        centre = centre_sums
    corrected = field.transpose(1, 0, 2).reshape(PCS, TILES_X, TILES_Y, CELLS_DEV)
    return (corrected, unit_rows(centre))
```

```python
import functools

import jax
import jax.numpy as jnp
from jax import lax
from jax.experimental import pallas as pl
from jax.experimental.pallas import tpu as pltpu
from jax.sharding import PartitionSpec as P

SLIDES = 40
SLOTS = 4
ITERS = 2
CLUSTERS = 100
PCS = 50
BOUND = 128
SHARPNESS = 20.0

LANES = 128
ROWS = 64
SENT = 56
ID_LANE = 126
LIVE_LANE = 127
NONE = -1000.0

F32 = jnp.float32
BF16 = jnp.bfloat16
HIGH = lax.Precision.HIGHEST
MESH = pl.DeviceIdType.MESH

NN = (((1,), (0,)), ((), ()))
NT = (((1,), (1,)), ((), ()))
TN = (((0,), (0,)), ((), ()))


def dot(a, b, dims):
    return lax.dot_general(a, b, dims, preferred_element_type=F32)


def dot_f32(a, b, dims):
    return lax.dot_general(a, b, dims, precision=HIGH, preferred_element_type=F32)


def split2(v):
    hi = v.astype(BF16)
    return hi, (v - hi.astype(F32)).astype(BF16)


def dot3(a, b, dims):
    ah, al = a if isinstance(a, tuple) else split2(a)
    bh, bl = split2(b)
    return dot(ah, bh, dims) + (dot(ah, bl, dims) + dot(al, bh, dims))


def iota(shape, dim):
    return lax.broadcasted_iota(jnp.int32, shape, dim)


class Sizes:
    def __init__(self, nx, ny):
        self.nx, self.ny = nx, ny
        self.gx = 8 if ny % 8 == 0 else 2
        self.gy = ny // self.gx
        self.dp = -(-PCS // ny)
        self.cr = self.dp * 8
        self.dense = (self.dp + 1) * SLIDES + self.dp
        self.dr = -(-self.dense // (nx * 8)) * 8
        self.drt = self.dr * nx


def kernel(
    sz, emb, nbr, sid, live, cent, out, outc,
    own, nb, cmat, zs, whi, wlo, cpad, e0, e2,
    f0, r0, f1, r1, f2, r2, s1, q1, s2, q2, s3, q3, s4, q4,
    halo_s, halo_r, ss, rs,
):
    nx, ny, gx, gy, dp, cr, dr = sz.nx, sz.ny, sz.gx, sz.gy, sz.dp, sz.cr, sz.dr
    cells = own.shape[1] - 8 * BOUND
    x, y = lax.axis_index("tx"), lax.axis_index("ty")

    def on_tx(r):
        return (lax.rem(x + r, nx), y)

    def on_ty(r):
        return (x, lax.rem(y + r, ny))

    def on_near(r):
        return (x, (y // gx) * gx + lax.rem(lax.rem(y, gx) + r, gx))

    def on_far(r):
        return (x, lax.rem(y + r * gx, ny))

    bar = pltpu.get_barrier_semaphore()

    def greet_ty(r, c):
        pl.semaphore_signal(bar, inc=1, device_id=on_ty(r), device_id_type=MESH)
        return c

    def greet_tx(r, c):
        pl.semaphore_signal(bar, inc=1, device_id=on_tx(r), device_id_type=MESH)
        return c

    lax.fori_loop(1, nx, greet_tx, 0)
    lax.fori_loop(1, ny, greet_ty, 0)
    for a in (1, nx - 1):
        for b in (1, ny - 1):
            pl.semaphore_signal(
                bar, inc=1, device_id=(lax.rem(x + a, nx), lax.rem(y + b, ny)), device_id_type=MESH
            )

    own[PCS:, :cells] = jnp.zeros((ROWS - PCS, cells), F32)
    own[:PCS, :cells] = emb[:, 0, 0, :]
    r0[:, :, SLOTS:, :] = jnp.zeros((ITERS, nx, 8 - SLOTS, LANES), F32)
    ids = nbr[:, 0, 0, :]
    center = 5 * BOUND + cells - BOUND
    ids = jnp.where(ids < center, ids, jnp.where(ids < center + BOUND, ids - center, ids - BOUND))
    for n in range(ids.shape[0]):
        nb[n] = jnp.broadcast_to(ids[n : n + 1, :], (8, cells))
    rows8 = iota((8, cells), 0)

    def count(g, c):
        base = rows8 + g * 16
        low = jnp.zeros((8, cells), F32)
        high = jnp.zeros((8, cells), F32)
        for n in range(ids.shape[0]):
            here = nb[n]
            low = low + jnp.where(here == base, 1.0, 0.0)
            high = high + jnp.where(here == base + 8, 1.0, 0.0)
        at = pl.multiple_of(g * 16, 16)
        cmat[pl.ds(at, 16), :] = jnp.concatenate([low, high], axis=0).astype(BF16)
        return c

    groups = cmat.shape[0] // 16
    lax.fori_loop(0, groups * 5 // 8, count, 0)

    pl.semaphore_wait(bar, nx - 1 + ny - 1 + 4)

    place = 0
    for a in (-1, 0, 1):
        for b in (-1, 0, 1):
            if a == 0 and b == 0:
                continue
            to = (lax.rem(x - a + nx, nx), lax.rem(y - b + ny, ny))
            pltpu.make_async_remote_copy(
                src_ref=own.at[pl.ds(0, SENT), pl.ds(0, BOUND)],
                dst_ref=own.at[pl.ds(0, SENT), pl.ds(cells + place * BOUND, BOUND)],
                send_sem=halo_s,
                recv_sem=halo_r,
                device_id=to,
                device_id_type=MESH,
            ).start()
            place += 1

    lax.fori_loop(groups * 5 // 8, groups, count, 0)

    alive = iota((1, cells), 1) < live[...]
    livef = alive.astype(F32)
    slides = sid[0].astype(F32)
    left = jnp.where(alive, slides, 64.0)
    masks, names = [], []
    for _ in range(SLOTS):
        name = jnp.min(left, axis=1, keepdims=True)
        masks.append(jnp.where(left == name, livef, 0.0))
        names.append(jnp.where(name < 64.0, name, NONE))
        left = jnp.where(left > name, left, 64.0)
    row = iota((8, cells), 0)
    zero = jnp.zeros((8, cells), F32)

    def stack(parts, first):
        total = zero
        for i, part in enumerate(parts):
            total = total + jnp.where(row == first + i, part, 0.0)
        return total

    mask8 = stack(masks, 0)
    masked = mask8 + stack([1.0 - livef], SLOTS)
    extra0 = stack(masks[:3], 5)
    extra1 = stack(masks[3:], 5)
    slot_row = iota((8, LANES), 0)
    slot_lane = iota((8, LANES), 1)
    name8 = jnp.full((8, LANES), NONE, F32)
    for i in range(SLOTS):
        name8 = jnp.where(slot_row == i, names[i], name8)
    here8 = (slot_lane.astype(F32) == name8).astype(F32)
    chunk_row = iota((cr, LANES), 0)
    chunk_lane = iota((cr, LANES), 1)
    chunk_name = jnp.zeros((cr, LANES), F32)
    for j in range(dp):
        for i in range(SLOTS):
            chunk_name = jnp.where(chunk_row == j * 8 + i, names[i], chunk_name)
    for i, at in enumerate((5, 6, 7, 13)):
        chunk_name = jnp.where(chunk_row == at, names[i], chunk_name)
    chunk_name = jnp.where(chunk_lane == ID_LANE, chunk_name, 0.0)

    cpad[...] = jnp.zeros_like(cpad)
    cpad[:CLUSTERS, :PCS] = cent[...]
    centre = cpad[...].T[:ROWS, :]

    pltpu.make_async_remote_copy(
        src_ref=own.at[pl.ds(0, SENT), pl.ds(cells, 8 * BOUND)],
        dst_ref=own.at[pl.ds(0, SENT), pl.ds(cells, 8 * BOUND)],
        send_sem=halo_s,
        recv_sem=halo_r,
        device_id=(x, lax.rem(y + 1, ny)),
        device_id_type=MESH,
    ).wait_recv()

    everything = own[...]
    part1 = everything.astype(BF16)
    rest = everything - part1.astype(F32)
    part2 = rest.astype(BF16)
    part3 = (rest - part2.astype(F32)).astype(BF16)
    summed = dot(jnp.concatenate([part1, part2, part3], axis=0), cmat[...], NN)
    summed = (summed[2 * ROWS :] + summed[ROWS : 2 * ROWS]) + summed[:ROWS]
    field = (everything[:, :cells] + summed) / (ids.shape[0] + 1.0)
    field = jnp.where(iota((ROWS, cells), 0) < PCS, field, 0.0) * livef

    cluster = iota((LANES, cells), 0)
    lane40 = iota((1, LANES), 1)

    def exchange(turn, phase, count_, begin, src, dst, to, region):
        sem = turn * 7 + phase

        def start(r, c):
            pltpu.make_async_remote_copy(
                src_ref=src(r), dst_ref=dst(r), send_sem=ss.at[sem], recv_sem=rs.at[sem],
                device_id=to(r), device_id_type=MESH,
            ).start()
            return c

        lax.fori_loop(1, count_, start, 0)
        return pltpu.make_async_remote_copy(
            src_ref=region, dst_ref=region, send_sem=ss.at[sem], recv_sem=rs.at[sem],
            device_id=to(1), device_id_type=MESH,
        )

    pending = []
    for turn in range(ITERS):
        unit_y = centre / jnp.sqrt(jnp.sum(centre * centre, axis=0, keepdims=True) + 1.0)
        inverse = 1.0 / jnp.sqrt(jnp.sum(field * field, axis=0, keepdims=True) + 1.0)
        unit_z = field * inverse
        zs[...] = field
        score = dot_f32(unit_y, unit_z, TN)
        raw = jnp.where(cluster < CLUSTERS, jnp.exp(SHARPNESS * (score - 1.0)), 0.0)
        first = raw * (livef / jnp.sum(raw, axis=0, keepdims=True))
        first = jnp.where(cluster == LIVE_LANE, livef, first)
        occ = dot_f32(mask8, first, NT)
        occ = jnp.where(slot_lane == ID_LANE, name8, occ)

        f0[turn] = occ
        r0[turn, 0, :SLOTS] = occ[:SLOTS]
        copy = exchange(
            turn, 0, nx, x,
            lambda r: f0.at[turn, pl.ds(0, SLOTS)],
            lambda r: r0.at[turn, r, pl.ds(0, SLOTS)],
            on_tx, r0.at[turn, pl.ds(1, nx - 1), pl.ds(0, SLOTS)],
        )

        m8 = mask8 + stack([inverse], SLOTS)

        def build(p, c):
            parts = []
            for j in range(dp):
                part = zs[pl.ds(p * dp + j, 1), :] * m8
                if j == 0:
                    part = part + extra0
                if j == 1:
                    part = part + extra1
                parts.append(part)
            both = jnp.concatenate(parts, axis=0)
            hi, lo = split2(both)
            at = pl.multiple_of(p * cr, cr)
            whi[pl.ds(at, cr), :] = hi
            wlo[pl.ds(at, cr), :] = lo
            return c

        lax.fori_loop(0, ny, build, 0)

        copy.wait_recv()
        pending.append(copy)
        got = r0[turn].reshape(nx * 8, LANES)
        if turn == 0:
            name = jnp.broadcast_to(got[:, ID_LANE : ID_LANE + 1], (nx * 8, LANES))
            lane = iota((nx * 8, LANES), 1).astype(F32)
            slot = lax.rem(iota((nx * 8, LANES), 0), 8)
            e0[...] = jnp.where((name == lane) & (slot < SLOTS), 1.0, 0.0).astype(BF16)
        hi, lo = split2(got)
        table = e0[...]
        part = (dot(table, lo, TN) + dot(table, hi, TN))[:SLIDES]
        f1[turn] = part
        r1[turn, 0] = part
        copy = exchange(
            turn, 1, gx, 0,
            lambda r: f1.at[turn],
            lambda r: r1.at[turn, r],
            on_near, r1.at[turn, pl.ds(1, gx - 1)],
        )
        copy.wait_recv()
        pending.append(copy)
        part = jnp.sum(r1[turn], axis=0)
        f2[turn] = part
        r2[turn, 0] = part
        copy = exchange(
            turn, 2, gy, 0,
            lambda r: f2.at[turn],
            lambda r: r2.at[turn, r],
            on_far, r2.at[turn, pl.ds(1, gy - 1)],
        )
        copy.wait_recv()
        pending.append(copy)
        occupied = jnp.sum(r2[turn], axis=0)
        totals = occupied[:, LIVE_LANE : LIVE_LANE + 1]
        expected = (
            jnp.sum(occupied, axis=0, keepdims=True)
            * totals
            / jnp.sum(totals, axis=0, keepdims=True)
        )
        ratio = (expected + 1.0) / (occupied + 1.0)
        ratio = jnp.where(lane40 < CLUSTERS, ratio * ratio, 1.0)
        mine = dot_f32(here8[:, :SLIDES], ratio, NN)
        mine = jnp.where(slot_row == SLOTS, 1.0, mine)
        weighted = raw * dot_f32(mine, masked, TN)
        assign = weighted * (livef / jnp.sum(weighted, axis=0, keepdims=True))

        ah, al = split2(assign)
        wide = dot(whi[...], jnp.concatenate([ah, al], axis=0), NT)
        sums = wide[:, :LANES] + (wide[:, LANES:] + dot(wlo[...], ah, NT))
        sums = sums.reshape(ny, cr, LANES) + chunk_name[None]
        s1[turn] = sums
        copy = exchange(
            turn, 3, ny, 0,
            lambda r: s1.at[turn, lax.rem(y + r, ny)],
            lambda r: q1.at[turn, r],
            on_ty, q1.at[turn, pl.ds(1, ny - 1)],
        )
        q1[turn, 0] = s1[turn, y]
        copy.wait_recv()
        pending.append(copy)
        got = q1[turn].reshape(ny * cr, LANES)
        if turn == 0:
            shape = (ny, cr, sz.drt)
            q = iota(shape, 1)
            j, c = q // 8, lax.rem(q, 8)
            named = (c < SLOTS) | ((j == 0) & (c > SLOTS)) | ((j == 1) & (c == 5))
            start = jnp.where(
                c < SLOTS,
                j * SLIDES,
                jnp.where(c == SLOTS, (dp + 1) * SLIDES + j, dp * SLIDES),
            ).astype(F32)
            name = got.reshape(ny, cr, LANES)[:, :, ID_LANE : ID_LANE + 1]
            goal = start + jnp.where(named, name, jnp.where(c == SLOTS, 0.0, NONE))
            table = jnp.where(goal == iota(shape, 2).astype(F32), 1.0, 0.0)
            e2[...] = table.reshape(ny * cr, sz.drt).astype(BF16)
        hi, lo = split2(got)
        table = e2[...]
        part = dot(table, lo, TN) + dot(table, hi, TN)
        s2[turn] = part.reshape(nx, dr, LANES)

        copy = exchange(
            turn, 4, nx, 0,
            lambda r: s2.at[turn, lax.rem(x + r, nx)],
            lambda r: q2.at[turn, r],
            on_tx, q2.at[turn, pl.ds(1, nx - 1)],
        )
        q2[turn, 0] = s2[turn, x]
        copy.wait_recv()
        pending.append(copy)
        part = jnp.sum(q2[turn], axis=0)
        s3[turn] = part
        q3[turn, x] = part
        copy = exchange(
            turn, 5, nx, 0,
            lambda r: s3.at[turn],
            lambda r: q3.at[turn, x],
            on_tx, q3.at[turn, pl.ds(1, nx - 1)],
        )
        copy.wait_recv()
        pending.append(copy)
        whole = q3[turn].reshape(sz.drt, LANES)
        counts = whole[dp * SLIDES : (dp + 1) * SLIDES]
        scale = 1.0 / (counts + 1.0)
        weight = jnp.sum(counts * scale, axis=0, keepdims=True)
        weight = jnp.where(lane40 < CLUSTERS, weight, 1.0)
        betas = []
        for j in range(dp):
            part = whole[j * SLIDES : (j + 1) * SLIDES]
            mean = jnp.sum(part * scale, axis=0, keepdims=True) / weight
            betas.append((part - counts * mean) * scale)
        betas.append(whole[dp * SLIDES :])
        hi, lo = split2(jnp.concatenate(betas, axis=0))
        chosen = dot(e2[...], jnp.concatenate([hi, lo], axis=1), NN)
        chosen = chosen[:, :LANES] + chosen[:, LANES:]
        s4[turn] = chosen.reshape(ny, cr, LANES)

        at = pl.multiple_of(y * cr, cr)
        copy = exchange(
            turn, 6, ny, 0,
            lambda r: s4.at[turn, r],
            lambda r: q4.at[turn, pl.ds(at, cr)],
            lambda r: on_ty(ny - r), q4.at[turn, pl.ds(cr, (ny - 1) * cr)],
        )
        q4[turn, pl.ds(at, cr)] = s4[turn, 0]
        copy.wait_recv()
        pending.append(copy)
        count_d = ny * dp
        slot_beta = [q4[turn, pl.ds(i, count_d, stride=8), :] for i in range(SLOTS)]
        shifts = dot3(jnp.concatenate(slot_beta, axis=0), assign, NN)
        shift = shifts[:count_d] * masks[0]
        for i in range(1, SLOTS):
            shift = shift + shifts[i * count_d : (i + 1) * count_d] * masks[i]
        centre = q4[turn, pl.ds(SLOTS, count_d, stride=8), :]
        if count_d < ROWS:
            shift = jnp.concatenate([shift, jnp.zeros((ROWS - count_d, cells), F32)], axis=0)
            centre = jnp.concatenate([centre, jnp.zeros((ROWS - count_d, LANES), F32)], axis=0)
        field = field - shift

    out[:, 0, 0, :] = field[:PCS]
    unit_y = centre / jnp.sqrt(jnp.sum(centre * centre, axis=0, keepdims=True) + 1.0)
    cpad[:ROWS, :] = unit_y
    outc[...] = cpad[...].T[:CLUSTERS, :PCS]

    pltpu.make_async_remote_copy(
        src_ref=own.at[pl.ds(0, SENT), pl.ds(cells, 8 * BOUND)],
        dst_ref=own.at[pl.ds(0, SENT), pl.ds(cells, 8 * BOUND)],
        send_sem=halo_s,
        recv_sem=halo_r,
        device_id=(x, lax.rem(y + 1, ny)),
        device_id_type=MESH,
    ).wait_send()
    for copy in pending:
        copy.wait_send()


def per_device(sz, embedding, neighbors, slide_id, live_count, centroids):
    cells = embedding.shape[3]
    near = neighbors.shape[0]
    nx, ny, cr, dr = sz.nx, sz.ny, sz.cr, sz.dr
    vmem = pl.BlockSpec(memory_space=pltpu.VMEM)

    def buf(*shape):
        return pltpu.VMEM((ITERS,) + shape, F32)

    return pl.pallas_call(
        functools.partial(kernel, sz),
        out_shape=(
            jax.ShapeDtypeStruct(embedding.shape, F32),
            jax.ShapeDtypeStruct(centroids.shape, F32),
        ),
        in_specs=[vmem] * 5,
        out_specs=(vmem, vmem),
        scratch_shapes=[
            pltpu.VMEM((ROWS, cells + 8 * BOUND), F32),
            pltpu.VMEM((near, 8, cells), jnp.int32),
            pltpu.VMEM((cells + 8 * BOUND, cells), BF16),
            pltpu.VMEM((ROWS, cells), F32),
            pltpu.VMEM((ny * cr, cells), BF16),
            pltpu.VMEM((ny * cr, cells), BF16),
            pltpu.VMEM((LANES, LANES), F32),
            pltpu.VMEM((nx * 8, LANES), BF16),
            pltpu.VMEM((ny * cr, sz.drt), BF16),
            buf(8, LANES),
            buf(nx, 8, LANES),
            buf(SLIDES, LANES),
            buf(sz.gx, SLIDES, LANES),
            buf(SLIDES, LANES),
            buf(sz.gy, SLIDES, LANES),
            buf(ny, cr, LANES),
            buf(ny, cr, LANES),
            buf(nx, dr, LANES),
            buf(nx, dr, LANES),
            buf(dr, LANES),
            buf(nx, dr, LANES),
            buf(ny, cr, LANES),
            buf(ny * cr, LANES),
            pltpu.SemaphoreType.DMA,
            pltpu.SemaphoreType.DMA,
            pltpu.SemaphoreType.DMA((7 * ITERS,)),
            pltpu.SemaphoreType.DMA((7 * ITERS,)),
        ],
        compiler_params=pltpu.CompilerParams(
            collective_id=0, has_side_effects=True, vmem_limit_bytes=48 * 1024 * 1024
        ),
        name="harmony",
    )(embedding, neighbors, slide_id, live_count, centroids)


def solution(mesh):
    sz = Sizes(mesh.shape["tx"], mesh.shape["ty"])
    placed = (
        P(None, "tx", "ty", None),
        P(None, "tx", "ty", None),
        P("tx", "ty", None),
        P("tx", "ty"),
        P(),
    )
    return jax.shard_map(
        functools.partial(per_device, sz),
        mesh=mesh,
        in_specs=placed,
        out_specs=(P(None, "tx", "ty", None), P()),
        check_vma=False,
    )
```

```python
import functools

import jax
import jax.numpy as jnp
from jax import lax
from jax.experimental import pallas as pl
from jax.experimental.pallas import tpu as pltpu
from jax.sharding import PartitionSpec as P

SLIDES = 40
SLOTS = 4
ITERS = 2
CLUSTERS = 100
PCS = 50
BOUND = 128
SHARPNESS = 20.0

LANES = 128
ROWS = 56
PAIRS = 25
CHUNK = 16
SENT = 14
BACK = 10
ID_LANE = 126
LIVE_LANE = 127
NONE = -1000.0

F32 = jnp.float32
BF16 = jnp.bfloat16
HIGH = lax.Precision.HIGHEST
MESH = pl.DeviceIdType.MESH

NN = (((1,), (0,)), ((), ()))
NT = (((1,), (1,)), ((), ()))
TN = (((0,), (0,)), ((), ()))


def dot(a, b, dims):
    return lax.dot_general(a, b, dims, preferred_element_type=F32)


def dot_f32(a, b, dims):
    return lax.dot_general(a, b, dims, precision=HIGH, preferred_element_type=F32)


def split2(v):
    hi = v.astype(BF16)
    return hi, (v - hi.astype(F32)).astype(BF16)


def dot3(a, b, dims):
    ah, al = a if isinstance(a, tuple) else split2(a)
    bh, bl = split2(b)
    return dot(ah, bh, dims) + (dot(ah, bl, dims) + dot(al, bh, dims))


def iota(shape, dim):
    return lax.broadcasted_iota(jnp.int32, shape, dim)


SIDE = 4


def ring(a):
    return min(a, SIDE - a)


SQUARE = sorted(
    ((a, b) for a in range(SIDE) for b in range(SIDE)), key=lambda o: -ring(o[0]) - ring(o[1])
)
OTHERS = [(a, b, c) for a, b in SQUARE for c in (1, 0) if a or b or c]
NEAR = [(0, b, c) for b in (2, 1, 3, 0) for c in (1, 0) if b or c]
FAR = [(a, 0, 0) for a in (2, 1, 3)]
DENSE = 3 * SLIDES + 2


def slot_of(a, b, c):
    return (a * SIDE + b) * 2 + c


def kernel(
    nx, ny, emb, nbr, sid, live, cent, out, outc,
    embv, nbrv, own, nb, cmat, zs, whi, wlo, cpad, e0, e2,
    f0, r0, f1, r1, f2, r2, s1, q1, s2, q2, s3, q3, s4, q4,
    load, halo_s, halo_r, ss, rs, seen,
):
    cells = own.shape[1] - 8 * BOUND
    dr = s2.shape[2]
    x, y = lax.axis_index("tx"), lax.axis_index("ty")
    core, chip = lax.rem(y, 2), y // 2
    chip_y, chip_x = chip // SIDE, lax.rem(chip, SIDE)
    pair = core * (SIDE * SIDE) + chip
    across = sorted(range(1, nx), key=lambda r: -min(r, nx - r))

    def on_tx(r):
        return (lax.rem(x + r, nx), y)

    def on_ty(a, b, c):
        to = lax.rem(chip_y + a, SIDE) * SIDE + lax.rem(chip_x + b, SIDE)
        return (x, to * 2 + lax.rem(core + c, 2))

    get_ids = pltpu.make_async_copy(nbr, nbrv, load.at[0])
    get_ids.start()
    get_emb = pltpu.make_async_copy(emb, embv, load.at[1])
    get_emb.start()

    bar = pltpu.get_barrier_semaphore()

    def tile(a, b):
        return (lax.rem(x + a + nx, nx), lax.rem(y + b + ny, ny))

    def greet(sem, a, b):
        pl.semaphore_signal(sem, inc=1, device_id=tile(a, b), device_id_type=MESH)

    border = [(a, b) for a in (-1, 0, 1) for b in (-1, 0, 1) if a or b]
    first_met = border + [(a, 0) for a in (-3, -2, 2, 3)]
    for a, b in first_met:
        greet(bar, a, b)

    def greet_tx(step, d):
        for a in (-d, d):
            greet(seen.at[step], a, 0)

    def greet_ty(step, d):
        for b in (-d, d):
            greet(seen.at[step], 0, b)

    def heard(step):
        pl.semaphore_wait(seen.at[step], 2)

    r0[:, :, SLOTS:, :] = jnp.zeros((ITERS, nx, 8 - SLOTS, LANES), F32)
    q1[:, :, SENT:, :] = jnp.zeros((ITERS, ny, CHUNK - SENT, LANES), F32)
    q4[:, PAIRS * BACK :, :] = jnp.zeros((ITERS, q4.shape[1] - PAIRS * BACK, LANES), F32)
    cpad[...] = jnp.zeros_like(cpad)
    cpad[:PCS, :CLUSTERS] = cent[...]
    own[PCS:, :cells] = jnp.zeros((ROWS - PCS, cells), F32)
    get_ids.wait()
    ids = nbrv[:, 0, 0, :]
    center = 5 * BOUND + cells - BOUND
    ids = jnp.where(ids < center, ids, jnp.where(ids < center + BOUND, ids - center, ids - BOUND))
    for n in range(ids.shape[0]):
        nb[n] = jnp.broadcast_to(ids[n : n + 1, :], (8, cells))
    rows8 = iota((8, cells), 0)

    def count(g, c):
        base = rows8 + g * 16
        low = jnp.zeros((8, cells), F32)
        high = jnp.zeros((8, cells), F32)
        for n in range(ids.shape[0]):
            here = nb[n]
            low = low + jnp.where(here == base, 1.0, 0.0)
            high = high + jnp.where(here == base + 8, 1.0, 0.0)
        at = pl.multiple_of(g * 16, 16)
        cmat[pl.ds(at, 16), :] = jnp.concatenate([low, high], axis=0).astype(BF16)
        return c

    groups = cmat.shape[0] // 16
    early = groups * 7 // 16
    lax.fori_loop(0, early, count, 0)
    get_emb.wait()
    own[:PCS, :cells] = embv[:, 0, 0, :]

    pl.semaphore_wait(bar, len(first_met))

    for place, (a, b) in enumerate(border):
        pltpu.make_async_remote_copy(
            src_ref=own.at[:, pl.ds(0, BOUND)],
            dst_ref=own.at[:, pl.ds(cells + place * BOUND, BOUND)],
            send_sem=halo_s,
            recv_sem=halo_r,
            device_id=tile(-a, -b),
            device_id_type=MESH,
        ).start()
    halo = pltpu.make_async_remote_copy(
        src_ref=own.at[:, pl.ds(cells, 8 * BOUND)],
        dst_ref=own.at[:, pl.ds(cells, 8 * BOUND)],
        send_sem=halo_s,
        recv_sem=halo_r,
        device_id=on_tx(1),
        device_id_type=MESH,
    )

    greet_tx(0, 3)
    greet_ty(2, 1)
    lax.fori_loop(early, groups, count, 0)

    alive = iota((1, cells), 1) < live[...]
    livef = alive.astype(F32)
    slides = sid[0].astype(F32)
    left = jnp.where(alive, slides, 64.0)
    masks, names = [], []
    for _ in range(SLOTS):
        name = jnp.min(left, axis=1, keepdims=True)
        masks.append(jnp.where(left == name, livef, 0.0))
        names.append(jnp.where(name < 64.0, name, NONE))
        left = jnp.where(left > name, left, 64.0)
    row = iota((8, cells), 0)

    def stack(parts):
        total = jnp.zeros((8, cells), F32)
        for at, part in parts:
            total = total + jnp.where(row == at, part, 0.0)
        return total

    by_slot = list(enumerate(masks))
    mask8 = stack(by_slot)
    masked = stack(by_slot + [(SLOTS, 1.0 - livef)])
    slot_row = iota((8, LANES), 0)
    slot_lane = iota((8, LANES), 1)
    name8 = jnp.full((8, LANES), NONE, F32)
    for i in range(SLOTS):
        name8 = jnp.where(slot_row == i, names[i], name8)
    here8 = (slot_lane.astype(F32) == name8).astype(F32)
    chunk_row = iota((CHUNK, LANES), 0)
    chunk_lane = iota((CHUNK, LANES), 1)
    chunk_name = jnp.zeros((CHUNK, LANES), F32)
    for first in (0, 5, 10):
        for i in range(SLOTS):
            chunk_name = jnp.where(chunk_row == first + i, names[i], chunk_name)
    chunk_name = jnp.where(chunk_lane == ID_LANE, chunk_name, 0.0)
    centre = cpad[...]

    heard(0)
    greet_tx(1, 2)
    heard(2)
    greet_ty(3, 2)
    halo.wait_recv()
    everything = own[...]
    part1 = everything.astype(BF16).astype(F32)
    rest = everything - part1
    part2 = rest.astype(BF16).astype(F32)
    parts = jnp.concatenate([part1, part2, rest - part2], axis=0).astype(BF16)
    summed = dot(parts, cmat[...], NN)
    summed = (summed[2 * ROWS :] + summed[ROWS : 2 * ROWS]) + summed[:ROWS]
    field = (everything[:, :cells] + summed) / (ids.shape[0] + 1.0)
    field = jnp.where(iota((ROWS, cells), 0) < PCS, field, 0.0) * livef

    heard(3)
    greet_ty(4, 4)
    heard(1)

    cluster = iota((LANES, cells), 0)
    lane40 = iota((1, LANES), 1)

    def sender(sem):
        def send(src, dst, to):
            pltpu.make_async_remote_copy(
                src_ref=src, dst_ref=dst, send_sem=ss.at[sem], recv_sem=rs.at[sem],
                device_id=to, device_id_type=MESH,
            ).start()

        return send

    def arrivals(sem, region):
        return pltpu.make_async_remote_copy(
            src_ref=region, dst_ref=region, send_sem=ss.at[sem], recv_sem=rs.at[sem],
            device_id=on_tx(1), device_id_type=MESH,
        )

    pending = []
    at_pairs = []
    for turn in range(ITERS):
        sem = turn * 7
        unit_y = centre / jnp.sqrt(jnp.sum(centre * centre, axis=0, keepdims=True) + 1.0)
        inverse = 1.0 / jnp.sqrt(jnp.sum(field * field, axis=0, keepdims=True) + 1.0)
        unit_z = field * inverse
        zs[...] = field
        score = dot_f32(unit_y, unit_z, TN)
        raw = jnp.where(cluster < CLUSTERS, jnp.exp(SHARPNESS * (score - 1.0)), 0.0)
        first = raw * (livef / jnp.sum(raw, axis=0, keepdims=True))
        first = jnp.where(cluster == LIVE_LANE, livef, first)
        occ = dot_f32(mask8, first, NT)
        occ = jnp.where(slot_lane == ID_LANE, name8, occ)

        f0[turn] = occ
        send = sender(sem)
        for r in across:
            send(f0.at[turn, pl.ds(0, SLOTS)], r0.at[turn, r, pl.ds(0, SLOTS)], on_tx(r))
        r0[turn, 0, :SLOTS] = occ[:SLOTS]

        if turn == 0:
            heard(4)
            greet_ty(5, 8)

        slots_a = stack(by_slot + [(4, inverse)] + [(5 + i, masks[i]) for i in range(3)])
        slots_b = stack([(0, masks[3]), (1, inverse)])
        ones_b = stack([(2 + i, masks[i]) for i in range(SLOTS)])

        def build(p, c):
            one = zs[pl.ds(p * 2, 1), :]
            two = zs[pl.ds(p * 2 + 1, 1), :]
            upper = jnp.where(row < 5, one, two) * slots_a
            lower = two * slots_b + ones_b
            hi, lo = split2(jnp.concatenate([upper, lower], axis=0))
            at = pl.multiple_of(p * CHUNK, CHUNK)
            whi[pl.ds(at, CHUNK), :] = hi
            wlo[pl.ds(at, CHUNK), :] = lo
            return c

        lax.fori_loop(0, PAIRS, build, 0)

        if turn == 0:
            heard(5)
        copy = arrivals(sem, r0.at[turn, pl.ds(1, nx - 1), pl.ds(0, SLOTS)])
        copy.wait_recv()
        pending.append(copy)
        got = r0[turn].reshape(nx * 8, LANES)
        if turn == 0:
            name = jnp.broadcast_to(got[:, ID_LANE : ID_LANE + 1], (nx * 8, LANES))
            lane = iota((nx * 8, LANES), 1).astype(F32)
            slot = lax.rem(iota((nx * 8, LANES), 0), 8)
            e0[...] = jnp.where((name == lane) & (slot < SLOTS), 1.0, 0.0).astype(BF16)
        hi, lo = split2(got)
        table = e0[...]
        part = (dot(table, lo, TN) + dot(table, hi, TN))[:SLIDES]
        f1[turn] = part
        send = sender(sem + 1)
        for offset in NEAR:
            send(f1.at[turn], r1.at[turn, slot_of(*offset)], on_ty(*offset))
        r1[turn, 0] = part
        copy = arrivals(sem + 1, r1.at[turn, pl.ds(1, len(NEAR))])
        copy.wait_recv()
        pending.append(copy)
        part = jnp.sum(r1[turn], axis=0)
        f2[turn] = part
        send = sender(sem + 2)
        for offset in FAR:
            send(f2.at[turn], r2.at[turn, offset[0]], on_ty(*offset))
        r2[turn, 0] = part
        copy = arrivals(sem + 2, r2.at[turn, pl.ds(1, len(FAR))])
        copy.wait_recv()
        pending.append(copy)
        occupied = jnp.sum(r2[turn], axis=0)
        totals = occupied[:, LIVE_LANE : LIVE_LANE + 1]
        expected = (
            jnp.sum(occupied, axis=0, keepdims=True)
            * totals
            / jnp.sum(totals, axis=0, keepdims=True)
        )
        ratio = (expected + 1.0) / (occupied + 1.0)
        ratio = jnp.where(lane40 < CLUSTERS, ratio * ratio, 1.0)
        mine = dot_f32(here8[:, :SLIDES], ratio, NN)
        mine = jnp.where(slot_row == SLOTS, 1.0, mine)
        weighted = raw * dot_f32(mine, masked, TN)
        assign = weighted * (livef / jnp.sum(weighted, axis=0, keepdims=True))

        ah, al = split2(assign)
        both = jnp.concatenate([ah, al], axis=0)
        send = sender(sem + 3)
        chips = SIDE * SIDE
        for side, count_ in ((0, chips), (1, PAIRS - chips)):
            rows = pl.ds(side * chips * CHUNK, count_ * CHUNK)
            wide = dot(whi[rows, :], both, NT)
            sums = wide[:, :LANES] + (wide[:, LANES:] + dot(wlo[rows, :], ah, NT))
            sums = sums.reshape(count_, CHUNK, LANES) + chunk_name[None]
            s1[turn, pl.ds(side * chips, count_)] = sums
            c = lax.rem(core + side, 2)
            for a, b in SQUARE:
                to = lax.rem(chip_y + a, SIDE) * SIDE + lax.rem(chip_x + b, SIDE)

                def go(a=a, b=b, to=to, c=c, side=side):
                    send(
                        s1.at[turn, side * chips + to, pl.ds(0, SENT)],
                        q1.at[turn, (a * SIDE + b) * 2 + c, pl.ds(0, SENT)],
                        (x, to * 2 + side),
                    )

                if side == 0 and (a or b):
                    go()
                elif side == 0:
                    pl.when(core != side)(go)
                elif a or b:
                    pl.when(to < count_)(go)
                else:
                    pl.when((core != side) & (to < count_))(go)

        @pl.when(pair < PAIRS)
        def _():
            q1[turn, 0, :SENT] = s1[turn, pair, :SENT]
            arrivals(sem + 3, q1.at[turn, pl.ds(1, ny - 1), pl.ds(0, SENT)]).wait_recv()
            got = q1[turn].reshape(ny * CHUNK, LANES)
            if turn == 0:
                shape = (ny * CHUNK, LANES)
                at = lax.rem(iota(shape, 0), CHUNK)
                second = (at >= 5) & (at < 10)
                middle = (at == 4) | (at == 9)
                start = jnp.where(
                    middle,
                    3 * SLIDES + second.astype(jnp.int32),
                    jnp.where(second, SLIDES, jnp.where(at >= 10, 2 * SLIDES, 0)),
                ).astype(F32)
                name = jnp.broadcast_to(got[:, ID_LANE : ID_LANE + 1], shape)
                name = jnp.where(middle, 0.0, jnp.where(at < SENT, name, NONE))
                goal = start + name
                table = jnp.where(goal == iota(shape, 1).astype(F32), 1.0, 0.0)
                e2[...] = table.astype(BF16)
            hi, lo = split2(got)
            table = e2[...]
            part = dot(table, lo, TN) + dot(table, hi, TN)
            s2[turn] = part.reshape(nx, dr, LANES)

            send = sender(sem + 4)
            for r in across:
                send(s2.at[turn, lax.rem(x + r, nx)], q2.at[turn, r], on_tx(r))
            q2[turn, 0] = s2[turn, x]
            arrivals(sem + 4, q2.at[turn, pl.ds(1, nx - 1)]).wait_recv()
            part = jnp.sum(q2[turn], axis=0)
            s3[turn] = part
            send = sender(sem + 5)
            for r in across:
                send(s3.at[turn], q3.at[turn, x], on_tx(r))
            q3[turn, x] = part
            arrivals(sem + 5, q3.at[turn, pl.ds(1, nx - 1)]).wait_recv()
            whole = q3[turn].reshape(nx * dr, LANES)
            counts = whole[2 * SLIDES : 3 * SLIDES]
            scale = 1.0 / (counts + 1.0)
            weight = jnp.sum(counts * scale, axis=0, keepdims=True)
            weight = jnp.where(lane40 < CLUSTERS, weight, 1.0)
            betas = []
            for j in range(2):
                part = whole[j * SLIDES : (j + 1) * SLIDES]
                mean = jnp.sum(part * scale, axis=0, keepdims=True) / weight
                betas.append((part - counts * mean) * scale)
            betas.append(whole[2 * SLIDES :])
            hi, lo = split2(jnp.concatenate(betas, axis=0))
            chosen = dot(e2[...], jnp.concatenate([hi, lo], axis=1), NN)
            chosen = chosen[:, :LANES] + chosen[:, LANES:]
            s4[turn] = chosen.reshape(ny, CHUNK, LANES)

            send = sender(sem + 6)
            for a, b, c in OTHERS:
                send(
                    s4.at[turn, slot_of(a, b, c), pl.ds(0, BACK)],
                    q4.at[turn, pl.ds(pair * BACK, BACK)],
                    on_ty(SIDE - a, SIDE - b, 2 - c),
                )
            q4[turn, pl.ds(pair * BACK, BACK)] = s4[turn, 0, :BACK]
            arrivals(sem + 6, q4.at[turn, pl.ds(0, (PAIRS - 1) * BACK)]).wait_recv()

        @pl.when(pair >= PAIRS)
        def _():
            arrivals(sem + 6, q4.at[turn, pl.ds(0, PAIRS * BACK)]).wait_recv()

        slot_beta = [q4[turn, pl.ds(i, ROWS, stride=5), :] for i in range(SLOTS)]
        shifts = dot3(jnp.concatenate(slot_beta, axis=0), assign, NN)
        for i in range(SLOTS):
            field = field - shifts[i * ROWS : (i + 1) * ROWS] * masks[i]
        centre = q4[turn, pl.ds(SLOTS, ROWS, stride=5), :]

    out[:, 0, 0, :] = field[:PCS]
    unit_y = centre / jnp.sqrt(jnp.sum(centre * centre, axis=0, keepdims=True) + 1.0)
    outc[...] = unit_y[:PCS, :CLUSTERS]

    halo.wait_send()
    for copy in pending:
        copy.wait_send()
    for turn in range(ITERS):
        sem = turn * 7

        @pl.when(pair < PAIRS)
        def _():
            arrivals(sem + 3, q1.at[turn, pl.ds(0, PAIRS - 1), pl.ds(0, SENT)]).wait_send()
            arrivals(sem + 4, q2.at[turn, pl.ds(1, nx - 1)]).wait_send()
            arrivals(sem + 5, q3.at[turn, pl.ds(1, nx - 1)]).wait_send()
            arrivals(sem + 6, s4.at[turn, pl.ds(1, ny - 1), pl.ds(0, BACK)]).wait_send()

        @pl.when(pair >= PAIRS)
        def _():
            arrivals(sem + 3, q1.at[turn, pl.ds(0, PAIRS), pl.ds(0, SENT)]).wait_send()


def per_device(nx, ny, embedding, neighbors, slide_id, live_count, centroids):
    cells = embedding.shape[3]
    near = neighbors.shape[0]
    dr = -(-DENSE // (nx * 8)) * 8
    vmem = pl.BlockSpec(memory_space=pltpu.VMEM)
    hbm = pl.BlockSpec(memory_space=pltpu.HBM)

    def buf(*shape):
        return pltpu.VMEM((ITERS,) + shape, F32)

    corrected, centers = pl.pallas_call(
        functools.partial(kernel, nx, ny),
        out_shape=(
            jax.ShapeDtypeStruct(embedding.shape, F32),
            jax.ShapeDtypeStruct((PCS, CLUSTERS), F32),
        ),
        in_specs=[hbm, hbm, vmem, vmem, vmem],
        out_specs=(vmem, vmem),
        scratch_shapes=[
            pltpu.VMEM(embedding.shape, F32),
            pltpu.VMEM(neighbors.shape, jnp.int32),
            pltpu.VMEM((ROWS, cells + 8 * BOUND), F32),
            pltpu.VMEM((near, 8, cells), jnp.int32),
            pltpu.VMEM((cells + 8 * BOUND, cells), BF16),
            pltpu.VMEM((ROWS, cells), F32),
            pltpu.VMEM((PAIRS * CHUNK, cells), BF16),
            pltpu.VMEM((PAIRS * CHUNK, cells), BF16),
            pltpu.VMEM((ROWS, LANES), F32),
            pltpu.VMEM((nx * 8, LANES), BF16),
            pltpu.VMEM((ny * CHUNK, LANES), BF16),
            buf(8, LANES),
            buf(nx, 8, LANES),
            buf(SLIDES, LANES),
            buf(len(NEAR) + 1, SLIDES, LANES),
            buf(SLIDES, LANES),
            buf(len(FAR) + 1, SLIDES, LANES),
            buf(PAIRS, CHUNK, LANES),
            buf(ny, CHUNK, LANES),
            buf(nx, dr, LANES),
            buf(nx, dr, LANES),
            buf(dr, LANES),
            buf(nx, dr, LANES),
            buf(ny, CHUNK, LANES),
            buf(ROWS * 5 + 8, LANES),
            pltpu.SemaphoreType.DMA((2,)),
            pltpu.SemaphoreType.DMA,
            pltpu.SemaphoreType.DMA,
            pltpu.SemaphoreType.DMA((7 * ITERS,)),
            pltpu.SemaphoreType.DMA((7 * ITERS,)),
            pltpu.SemaphoreType.REGULAR((6,)),
        ],
        compiler_params=pltpu.CompilerParams(
            collective_id=0, has_side_effects=True, vmem_limit_bytes=48 * 1024 * 1024
        ),
        name="harmony",
    )(embedding, neighbors, slide_id, live_count, centroids.T)
    return corrected, centers.T


def solution(mesh):
    nx, ny = mesh.shape["tx"], mesh.shape["ty"]
    placed = (
        P(None, "tx", "ty", None),
        P(None, "tx", "ty", None),
        P("tx", "ty", None),
        P("tx", "ty"),
        P(),
    )
    return jax.shard_map(
        functools.partial(per_device, nx, ny),
        mesh=mesh,
        in_specs=placed,
        out_specs=(P(None, "tx", "ty", None), P()),
        check_vma=False,
    )
```

```python
import functools

import jax
import jax.numpy as jnp
from jax import lax
from jax.experimental import pallas as pl
from jax.experimental.pallas import tpu as pltpu
from jax.sharding import PartitionSpec as P

SLIDES = 40
SLOTS = 4
ITERS = 2
CLUSTERS = 100
PCS = 50
BOUND = 128
SHARPNESS = 20.0

LANES = 128
ROWS = 56
PAIRS = 25
CHUNK = 16
SENT = 14
BACK = 10
HALF = 20
PADDED = 24
ID_LANE = 126
LIVE_LANE = 127
NONE = -1000.0

F32 = jnp.float32
BF16 = jnp.bfloat16
MESH = pl.DeviceIdType.MESH

NN = (((1,), (0,)), ((), ()))
NT = (((1,), (1,)), ((), ()))
TN = (((0,), (0,)), ((), ()))


def dot(a, b, dims):
    return lax.dot_general(a, b, dims, preferred_element_type=F32)


def split2(v):
    hi = v.astype(BF16)
    return hi, (v - hi.astype(F32)).astype(BF16)


def halves(v):
    return v[:, :LANES] + v[:, LANES:]


def split_lanes(v):
    return jnp.concatenate(split2(v), axis=1)


def parts_of(v):
    hi = v.astype(BF16).astype(F32)
    return hi, v - hi


def iota(shape, dim):
    return lax.broadcasted_iota(jnp.int32, shape, dim)


SIDE = 4


def ring(a):
    return min(a, SIDE - a)


SQUARE = sorted(
    ((a, b) for a in range(SIDE) for b in range(SIDE)), key=lambda o: -ring(o[0]) - ring(o[1])
)
OTHERS = [(a, b, c) for a, b in SQUARE for c in (1, 0) if a or b or c]
NEAR = [(0, b, c) for b in (2, 1, 3, 0) for c in (1, 0) if b or c]
FAR = [(a, 0, 0) for a in (2, 1, 3)]
DENSE = 3 * SLIDES + 2


def dense_row(name):
    return jnp.where(name >= HALF, name + (PADDED - HALF), name)


def place_of(a, b):
    at = (a + 1) * 3 + b + 1
    return at - (at > 4)


def slot_of(a, b, c):
    return (a * SIDE + b) * 2 + c


def kernel(
    nx, ny, emb, nbr, sid, live, cent, out, outc,
    embv, nbrv, sidv, centv, own, nb, cmat, zs, whi, wlo, cpad, e0, e2,
    f0, r0, f1, r1, f2, r2, f3, r3, s1, q1, s2, q2, s3, q3, s4, q4,
    load, halo_s, halo_r, ss, rs, seen,
):
    cells = own.shape[1] - 8 * BOUND
    dr = s2.shape[2]
    x, y = lax.axis_index("tx"), lax.axis_index("ty")
    core, chip = lax.rem(y, 2), y // 2
    chip_y, chip_x = chip // SIDE, lax.rem(chip, SIDE)
    pair = core * (SIDE * SIDE) + chip
    across = sorted(range(1, nx), key=lambda r: -min(r, nx - r))

    def on_tx(r):
        return (lax.rem(x + r, nx), y)

    def on_ty(a, b, c):
        to = lax.rem(chip_y + a, SIDE) * SIDE + lax.rem(chip_x + b, SIDE)
        return (x, to * 2 + lax.rem(core + c, 2))

    get_ids = pltpu.make_async_copy(nbr, nbrv, load.at[0])
    get_ids.start()
    get_emb = pltpu.make_async_copy(emb, embv, load.at[1])
    get_emb.start()
    get_sid = pltpu.make_async_copy(sid, sidv, load.at[2])
    get_sid.start()
    get_cent = pltpu.make_async_copy(cent, centv, load.at[3])
    get_cent.start()

    bar = pltpu.get_barrier_semaphore()

    def tile(a, b):
        return (lax.rem(x + a + nx, nx), lax.rem(y + b + ny, ny))

    def greet(sem, a, b):
        pl.semaphore_signal(sem, inc=1, device_id=tile(a, b), device_id_type=MESH)

    border = [(a, b) for a in (-1, 1) for b in (-1, 1)] + [(-1, 0), (1, 0), (0, -1), (0, 1)]
    first_met = border + [(a, 0) for a in (-3, -2, 2, 3)]
    for a, b in first_met:
        greet(bar, a, b)

    def greet_tx(step, d):
        for a in (-d, d):
            greet(seen.at[step], a, 0)

    def greet_ty(step, d):
        for b in (-d, d):
            greet(seen.at[step], 0, b)

    def heard(step):
        pl.semaphore_wait(seen.at[step], 2)

    r0[:, :, SLOTS:, :] = jnp.zeros((ITERS, nx, 8 - SLOTS, LANES), F32)
    r1[:, HALF:, :] = jnp.zeros((ITERS, PADDED - HALF, LANES), F32)
    r2[:, :, HALF:, :] = jnp.zeros((ITERS, SIDE * SIDE, PADDED - HALF, LANES), F32)
    r3[:, :, HALF:, :] = jnp.zeros((ITERS, 2, PADDED - HALF, LANES), F32)
    q1[:, :, SENT:, :] = jnp.zeros((ITERS, ny, CHUNK - SENT, LANES), F32)
    q4[:, PAIRS * BACK :, :] = jnp.zeros((ITERS, q4.shape[1] - PAIRS * BACK, LANES), F32)
    cpad[...] = jnp.zeros_like(cpad)
    own[PCS:, :cells] = jnp.zeros((ROWS - PCS, cells), F32)
    get_ids.wait()
    ids = nbrv[:, 0, 0, :]
    center = 5 * BOUND + cells - BOUND
    ids = jnp.where(ids < center, ids, jnp.where(ids < center + BOUND, ids - center, ids - BOUND))
    for n in range(ids.shape[0]):
        nb[n] = jnp.broadcast_to(ids[n : n + 1, :], (8, cells))
    rows8 = iota((8, cells), 0)

    def count(g, c):
        base = rows8 + g * 16
        low = jnp.zeros((8, cells), F32)
        high = jnp.zeros((8, cells), F32)
        for n in range(ids.shape[0]):
            here = nb[n]
            low = low + jnp.where(here == base, 1.0, 0.0)
            high = high + jnp.where(here == base + 8, 1.0, 0.0)
        at = pl.multiple_of(g * 16, 16)
        cmat[pl.ds(at, 16), :] = jnp.concatenate([low, high], axis=0).astype(BF16)
        return c

    groups = cmat.shape[0] // 16
    early = groups * 10 // 16
    lax.fori_loop(0, early, count, 0)
    get_emb.wait()
    own[:PCS, :cells] = embv[:, 0, 0, :]

    pl.semaphore_wait(bar, len(first_met))

    for a, b in border:
        pltpu.make_async_remote_copy(
            src_ref=own.at[:, pl.ds(0, BOUND)],
            dst_ref=own.at[:, pl.ds(cells + place_of(a, b) * BOUND, BOUND)],
            send_sem=halo_s,
            recv_sem=halo_r,
            device_id=tile(-a, -b),
            device_id_type=MESH,
        ).start()
    halo = pltpu.make_async_remote_copy(
        src_ref=own.at[:, pl.ds(cells, 8 * BOUND)],
        dst_ref=own.at[:, pl.ds(cells, 8 * BOUND)],
        send_sem=halo_s,
        recv_sem=halo_r,
        device_id=on_tx(1),
        device_id_type=MESH,
    )

    greet_tx(0, 3)
    greet_ty(2, 1)
    lax.fori_loop(early, groups, count, 0)

    alive = iota((1, cells), 1) < live[...]
    livef = alive.astype(F32)
    get_sid.wait()
    slides = sidv[0].astype(F32)
    left = jnp.where(alive, slides, 64.0)
    masks, names = [], []
    for _ in range(SLOTS):
        name = jnp.min(left, axis=1, keepdims=True)
        masks.append(jnp.where(left == name, livef, 0.0))
        names.append(jnp.where(name < 64.0, name, NONE))
        left = jnp.where(left > name, left, 64.0)
    row = iota((8, cells), 0)

    def stack(parts):
        total = jnp.zeros((8, cells), F32)
        for at, part in parts:
            total = total + jnp.where(row == at, part, 0.0)
        return total

    by_slot = list(enumerate(masks))
    mask8 = stack(by_slot)
    mask8_bf = mask8.astype(BF16)
    masked = stack(by_slot + [(SLOTS, 1.0 - livef)])
    masked2 = jnp.concatenate([masked, masked], axis=0).astype(BF16)
    slot_row = iota((8, LANES), 0)
    slot_lane = iota((8, LANES), 1)
    name8 = jnp.full((8, LANES), NONE, F32)
    for i in range(SLOTS):
        name8 = jnp.where(slot_row == i, dense_row(names[i]), name8)
    here8_bf = jnp.where(slot_lane.astype(F32) == name8, 1.0, 0.0)[:, : 2 * PADDED].astype(BF16)
    chunk_row = iota((CHUNK, LANES), 0)
    chunk_lane = iota((CHUNK, LANES), 1)
    chunk_name = jnp.zeros((CHUNK, LANES), F32)
    for first in (0, 5, 10):
        for i in range(SLOTS):
            chunk_name = jnp.where(chunk_row == first + i, names[i], chunk_name)
    chunk_name = jnp.where(chunk_lane == ID_LANE, chunk_name, 0.0)
    get_cent.wait()
    cpad[:PCS, :CLUSTERS] = centv[...]
    centre = cpad[...]

    heard(0)
    greet_tx(1, 2)
    heard(2)
    greet_ty(3, 2)
    halo.wait_recv()
    everything = own[...]
    part1 = everything.astype(BF16).astype(F32)
    rest = everything - part1
    part2 = rest.astype(BF16).astype(F32)
    parts = jnp.concatenate([part1, part2, rest - part2], axis=0).astype(BF16)
    summed = dot(parts, cmat[...], NN)
    summed = (summed[2 * ROWS :] + summed[ROWS : 2 * ROWS]) + summed[:ROWS]
    field = (everything[:, :cells] + summed) / (ids.shape[0] + 1.0)
    field = jnp.where(iota((ROWS, cells), 0) < PCS, field, 0.0) * livef

    heard(3)
    greet_ty(4, 4)
    heard(1)

    cluster = iota((LANES, cells), 0)
    lane40 = iota((1, LANES), 1)

    def sender(sem):
        def send(src, dst, to):
            pltpu.make_async_remote_copy(
                src_ref=src, dst_ref=dst, send_sem=ss.at[sem], recv_sem=rs.at[sem],
                device_id=to, device_id_type=MESH,
            ).start()

        return send

    def arrivals(sem, region):
        return pltpu.make_async_remote_copy(
            src_ref=region, dst_ref=region, send_sem=ss.at[sem], recv_sem=rs.at[sem],
            device_id=on_tx(1), device_id_type=MESH,
        )

    pending = []
    at_pairs = []
    for turn in range(ITERS):
        sem = turn * 8
        unit_y = centre * lax.rsqrt(jnp.sum(centre * centre, axis=0, keepdims=True) + 1.0)
        inverse = lax.rsqrt(jnp.sum(field * field, axis=0, keepdims=True) + 1.0)
        unit_z = field * inverse
        zs[...] = field
        yh, yl = parts_of(unit_y)
        zh, zl = parts_of(unit_z)
        score = dot(
            jnp.concatenate([yh, yh, yl, yl], axis=0).astype(BF16),
            jnp.concatenate([zh, zl, zh, zl], axis=0).astype(BF16),
            TN,
        )
        raw = jnp.where(cluster < CLUSTERS, jnp.exp(SHARPNESS * (score - 1.0)), 0.0)
        first = raw * (livef / jnp.sum(raw, axis=0, keepdims=True))
        first = jnp.where(cluster == LIVE_LANE, livef, first)
        occ = halves(dot(mask8_bf, jnp.concatenate(split2(first), axis=0), NT))
        occ = jnp.where(slot_lane == ID_LANE, name8, occ)

        f0[turn] = occ
        send = sender(sem)
        for r in across:
            send(f0.at[turn, pl.ds(0, SLOTS)], r0.at[turn, r, pl.ds(0, SLOTS)], on_tx(r))
        r0[turn, 0, :SLOTS] = occ[:SLOTS]

        if turn == 0:
            heard(4)
            greet_ty(5, 8)

        slots_a = stack(by_slot + [(4, inverse)] + [(5 + i, masks[i]) for i in range(3)])
        slots_b = stack([(0, masks[3]), (1, inverse)])
        ones_b = stack([(2 + i, masks[i]) for i in range(SLOTS)])

        def build(p, c):
            one = zs[pl.ds(p * 2, 1), :]
            two = zs[pl.ds(p * 2 + 1, 1), :]
            upper = jnp.where(row < 5, one, two) * slots_a
            lower = two * slots_b + ones_b
            hi, lo = split2(jnp.concatenate([upper, lower], axis=0))
            at = pl.multiple_of(p * CHUNK, CHUNK)
            whi[pl.ds(at, CHUNK), :] = hi
            wlo[pl.ds(at, CHUNK), :] = lo
            return c

        lax.fori_loop(0, PAIRS, build, 0)

        if turn == 0:
            heard(5)
        copy = arrivals(sem, r0.at[turn, pl.ds(1, nx - 1), pl.ds(0, SLOTS)])
        copy.wait_recv()
        pending.append(copy)
        got = r0[turn].reshape(nx * 8, LANES)
        if turn == 0:
            name = jnp.broadcast_to(got[:, ID_LANE : ID_LANE + 1], (nx * 8, LANES))
            lane = iota((nx * 8, LANES), 1).astype(F32)
            slot = lax.rem(iota((nx * 8, LANES), 0), 8)
            e0[...] = jnp.where((name == lane) & (slot < SLOTS), 1.0, 0.0).astype(BF16)
        part = halves(dot(e0[...], split_lanes(got), TN)[: 2 * PADDED])
        f1[turn] = part.reshape(2, PADDED, LANES)
        send = sender(sem + 1)
        send(f1.at[turn, 1 - core, pl.ds(0, HALF)], r1.at[turn, pl.ds(0, HALF)], on_ty(0, 0, 1))
        copy = arrivals(sem + 1, r1.at[turn, pl.ds(0, HALF)])
        copy.wait_recv()
        pending.append(copy)
        part = r1[turn] + f1[turn, core]
        f2[turn] = part
        send = sender(sem + 2)
        for a, b in SQUARE[:-1]:
            send(
                f2.at[turn, pl.ds(0, HALF)],
                r2.at[turn, a * SIDE + b, pl.ds(0, HALF)],
                on_ty(a, b, 0),
            )
        r2[turn, 0] = part
        copy = arrivals(sem + 2, r2.at[turn, pl.ds(1, SIDE * SIDE - 1), pl.ds(0, HALF)])
        copy.wait_recv()
        pending.append(copy)
        part = jnp.sum(r2[turn], axis=0)
        f3[turn] = part
        send = sender(sem + 7)
        send(f3.at[turn, pl.ds(0, HALF)], r3.at[turn, core, pl.ds(0, HALF)], on_ty(0, 0, 1))
        r3[turn, core] = part
        copy = arrivals(sem + 7, r3.at[turn, 0, pl.ds(0, HALF)])
        copy.wait_recv()
        pending.append(copy)
        occupied = r3[turn].reshape(2 * PADDED, LANES)
        totals = occupied[:, LIVE_LANE : LIVE_LANE + 1]
        expected = (
            jnp.sum(occupied, axis=0, keepdims=True)
            * totals
            / jnp.sum(totals, axis=0, keepdims=True)
        )
        ratio = (expected + 1.0) / (occupied + 1.0)
        ratio = jnp.where(lane40 < CLUSTERS, ratio * ratio, 1.0)
        mine = dot(here8_bf, split_lanes(ratio), NN)
        mine_hi = jnp.where(slot_row == SLOTS, 1.0, mine[:, :LANES])
        mine2 = jnp.concatenate([mine_hi, mine[:, LANES:]], axis=0).astype(BF16)
        weighted = raw * dot(mine2, masked2, TN)
        assign = weighted * (livef / jnp.sum(weighted, axis=0, keepdims=True))

        ah, al = split2(assign)
        both = jnp.concatenate([ah, al], axis=0)
        send = sender(sem + 3)
        chips = SIDE * SIDE
        for side, count_ in ((0, chips), (1, PAIRS - chips)):
            rows = pl.ds(side * chips * CHUNK, count_ * CHUNK)
            wide = dot(whi[rows, :], both, NT)
            sums = halves(wide) + dot(wlo[rows, :], ah, NT)
            sums = sums.reshape(count_, CHUNK, LANES) + chunk_name[None]
            s1[turn, pl.ds(side * chips, count_)] = sums
            c = lax.rem(core + side, 2)
            for a, b in SQUARE:
                to = lax.rem(chip_y + a, SIDE) * SIDE + lax.rem(chip_x + b, SIDE)

                def go(a=a, b=b, to=to, c=c, side=side):
                    send(
                        s1.at[turn, side * chips + to, pl.ds(0, SENT)],
                        q1.at[turn, (a * SIDE + b) * 2 + c, pl.ds(0, SENT)],
                        (x, to * 2 + side),
                    )

                if side == 0 and (a or b):
                    go()
                elif side == 0:
                    pl.when(core != side)(go)
                elif a or b:
                    pl.when(to < count_)(go)
                else:
                    pl.when((core != side) & (to < count_))(go)

        @pl.when(pair < PAIRS)
        def _():
            q1[turn, 0, :SENT] = s1[turn, pair, :SENT]
            arrivals(sem + 3, q1.at[turn, pl.ds(1, ny - 1), pl.ds(0, SENT)]).wait_recv()
            got = q1[turn].reshape(ny * CHUNK, LANES)
            if turn == 0:
                shape = (ny * CHUNK, LANES)
                at = lax.rem(iota(shape, 0), CHUNK)
                second = (at >= 5) & (at < 10)
                middle = (at == 4) | (at == 9)
                start = jnp.where(
                    middle,
                    3 * SLIDES + second.astype(jnp.int32),
                    jnp.where(second, SLIDES, jnp.where(at >= 10, 2 * SLIDES, 0)),
                ).astype(F32)
                name = jnp.broadcast_to(got[:, ID_LANE : ID_LANE + 1], shape)
                name = jnp.where(middle, 0.0, jnp.where(at < SENT, name, NONE))
                goal = start + name
                table = jnp.where(goal == iota(shape, 1).astype(F32), 1.0, 0.0)
                e2[...] = table.astype(BF16)
            part = halves(dot(e2[...], split_lanes(got), TN))
            s2[turn] = part.reshape(nx, dr, LANES)

            send = sender(sem + 4)
            for r in across:
                send(s2.at[turn, lax.rem(x + r, nx)], q2.at[turn, r], on_tx(r))
            q2[turn, 0] = s2[turn, x]
            arrivals(sem + 4, q2.at[turn, pl.ds(1, nx - 1)]).wait_recv()
            part = jnp.sum(q2[turn], axis=0)
            s3[turn] = part
            send = sender(sem + 5)
            for r in across:
                send(s3.at[turn], q3.at[turn, x], on_tx(r))
            q3[turn, x] = part
            arrivals(sem + 5, q3.at[turn, pl.ds(1, nx - 1)]).wait_recv()
            whole = q3[turn].reshape(nx * dr, LANES)
            counts = whole[2 * SLIDES : 3 * SLIDES]
            scale = 1.0 / (counts + 1.0)
            weight = jnp.sum(counts * scale, axis=0, keepdims=True)
            weight = jnp.where(lane40 < CLUSTERS, weight, 1.0)
            betas = []
            for j in range(2):
                part = whole[j * SLIDES : (j + 1) * SLIDES]
                mean = jnp.sum(part * scale, axis=0, keepdims=True) / weight
                betas.append((part - counts * mean) * scale)
            betas.append(whole[2 * SLIDES :])
            chosen = halves(dot(e2[...], split_lanes(jnp.concatenate(betas, axis=0)), NN))
            s4[turn] = chosen.reshape(ny, CHUNK, LANES)

            send = sender(sem + 6)
            for a, b, c in OTHERS:
                send(
                    s4.at[turn, slot_of(a, b, c), pl.ds(0, BACK)],
                    q4.at[turn, pl.ds(pair * BACK, BACK)],
                    on_ty(SIDE - a, SIDE - b, 2 - c),
                )
            q4[turn, pl.ds(pair * BACK, BACK)] = s4[turn, 0, :BACK]
            arrivals(sem + 6, q4.at[turn, pl.ds(0, (PAIRS - 1) * BACK)]).wait_recv()

        @pl.when(pair >= PAIRS)
        def _():
            arrivals(sem + 6, q4.at[turn, pl.ds(0, PAIRS * BACK)]).wait_recv()

        slot_beta = [q4[turn, pl.ds(i, ROWS, stride=5), :] for i in range(SLOTS)]
        bh, bl = split2(jnp.concatenate(slot_beta, axis=0))
        shifts = dot(jnp.concatenate([bh, bh], axis=1), both, NN) + dot(bl, ah, NN)
        for i in range(SLOTS):
            field = field - shifts[i * ROWS : (i + 1) * ROWS] * masks[i]
        centre = q4[turn, pl.ds(SLOTS, ROWS, stride=5), :]

    out[:, 0, 0, :] = field[:PCS]
    unit_y = centre / jnp.sqrt(jnp.sum(centre * centre, axis=0, keepdims=True) + 1.0)
    outc[...] = unit_y[:PCS, :CLUSTERS]

    halo.wait_send()
    for copy in pending:
        copy.wait_send()
    for turn in range(ITERS):
        sem = turn * 8

        @pl.when(pair < PAIRS)
        def _():
            arrivals(sem + 3, q1.at[turn, pl.ds(0, PAIRS - 1), pl.ds(0, SENT)]).wait_send()
            arrivals(sem + 4, q2.at[turn, pl.ds(1, nx - 1)]).wait_send()
            arrivals(sem + 5, q3.at[turn, pl.ds(1, nx - 1)]).wait_send()
            arrivals(sem + 6, s4.at[turn, pl.ds(1, ny - 1), pl.ds(0, BACK)]).wait_send()

        @pl.when(pair >= PAIRS)
        def _():
            arrivals(sem + 3, q1.at[turn, pl.ds(0, PAIRS), pl.ds(0, SENT)]).wait_send()


def per_device(nx, ny, embedding, neighbors, slide_id, live_count, centroids):
    cells = embedding.shape[3]
    near = neighbors.shape[0]
    dr = -(-DENSE // (nx * 8)) * 8
    vmem = pl.BlockSpec(memory_space=pltpu.VMEM)
    hbm = pl.BlockSpec(memory_space=pltpu.HBM)

    def far(v):
        return pltpu.with_memory_space_constraint(v, pltpu.HBM)

    def buf(*shape):
        return pltpu.VMEM((ITERS,) + shape, F32)

    corrected, centers = pl.pallas_call(
        functools.partial(kernel, nx, ny),
        out_shape=(
            jax.ShapeDtypeStruct(embedding.shape, F32),
            jax.ShapeDtypeStruct((PCS, CLUSTERS), F32),
        ),
        in_specs=[hbm, hbm, hbm, vmem, hbm],
        out_specs=(vmem, vmem),
        scratch_shapes=[
            pltpu.VMEM(embedding.shape, F32),
            pltpu.VMEM(neighbors.shape, jnp.int32),
            pltpu.VMEM(slide_id.shape, jnp.int32),
            pltpu.VMEM((PCS, CLUSTERS), F32),
            pltpu.VMEM((ROWS, cells + 8 * BOUND), F32),
            pltpu.VMEM((near, 8, cells), jnp.int32),
            pltpu.VMEM((cells + 8 * BOUND, cells), BF16),
            pltpu.VMEM((ROWS, cells), F32),
            pltpu.VMEM((PAIRS * CHUNK, cells), BF16),
            pltpu.VMEM((PAIRS * CHUNK, cells), BF16),
            pltpu.VMEM((ROWS, LANES), F32),
            pltpu.VMEM((nx * 8, LANES), BF16),
            pltpu.VMEM((ny * CHUNK, LANES), BF16),
            buf(8, LANES),
            buf(nx, 8, LANES),
            buf(2, PADDED, LANES),
            buf(PADDED, LANES),
            buf(PADDED, LANES),
            buf(SIDE * SIDE, PADDED, LANES),
            buf(PADDED, LANES),
            buf(2, PADDED, LANES),
            buf(PAIRS, CHUNK, LANES),
            buf(ny, CHUNK, LANES),
            buf(nx, dr, LANES),
            buf(nx, dr, LANES),
            buf(dr, LANES),
            buf(nx, dr, LANES),
            buf(ny, CHUNK, LANES),
            buf(ROWS * 5 + 8, LANES),
            pltpu.SemaphoreType.DMA((4,)),
            pltpu.SemaphoreType.DMA,
            pltpu.SemaphoreType.DMA,
            pltpu.SemaphoreType.DMA((8 * ITERS,)),
            pltpu.SemaphoreType.DMA((8 * ITERS,)),
            pltpu.SemaphoreType.REGULAR((6,)),
        ],
        compiler_params=pltpu.CompilerParams(
            collective_id=0, has_side_effects=True, vmem_limit_bytes=48 * 1024 * 1024
        ),
        name="harmony",
    )(far(embedding), far(neighbors), far(slide_id), live_count, far(centroids.T))
    return corrected, centers.T


def solution(mesh):
    nx, ny = mesh.shape["tx"], mesh.shape["ty"]
    placed = (
        P(None, "tx", "ty", None),
        P(None, "tx", "ty", None),
        P("tx", "ty", None),
        P("tx", "ty"),
        P(),
    )
    return jax.shard_map(
        functools.partial(per_device, nx, ny),
        mesh=mesh,
        in_specs=placed,
        out_specs=(P(None, "tx", "ty", None), P()),
        check_vma=False,
    )
```

```python
import functools

import jax
import jax.numpy as jnp
from jax import lax
from jax.experimental import pallas as pl
from jax.experimental.pallas import tpu as pltpu
from jax.sharding import PartitionSpec as P

SLIDES = 40
SLOTS = 4
ITERS = 2
CLUSTERS = 100
PCS = 50
BOUND = 128
SHARPNESS = 20.0

LANES = 128
ROWS = 56
PAIRS = 25
CHUNK = 16
SENT = 14
BACK = 10
HALF = 20
PADDED = 24
ID_LANE = 126
LIVE_LANE = 127
NONE = -1000.0

F32 = jnp.float32
BF16 = jnp.bfloat16
MESH = pl.DeviceIdType.MESH

NN = (((1,), (0,)), ((), ()))
NT = (((1,), (1,)), ((), ()))
TN = (((0,), (0,)), ((), ()))


def dot(a, b, dims):
    return lax.dot_general(a, b, dims, preferred_element_type=F32)


def split2(v):
    hi = v.astype(BF16)
    return hi, (v - hi.astype(F32)).astype(BF16)


def halves(v):
    return v[:, :LANES] + v[:, LANES:]


def split_lanes(v):
    return jnp.concatenate(split2(v), axis=1)


def parts_of(v):
    hi = v.astype(BF16).astype(F32)
    return hi, v - hi


def iota(shape, dim):
    return lax.broadcasted_iota(jnp.int32, shape, dim)


SIDE = 4


def ring(a):
    return min(a, SIDE - a)


SQUARE = sorted(
    ((a, b) for a in range(SIDE) for b in range(SIDE)), key=lambda o: -ring(o[0]) - ring(o[1])
)
OTHERS = [(a, b, c) for a, b in SQUARE for c in (1, 0) if a or b or c]
NEAR = [(0, b, c) for b in (2, 1, 3, 0) for c in (1, 0) if b or c]
FAR = [(a, 0, 0) for a in (2, 1, 3)]
DENSE = 3 * SLIDES + 2


def dense_row(name):
    return jnp.where(name >= HALF, name + (PADDED - HALF), name)


def place_of(a, b):
    at = (a + 1) * 3 + b + 1
    return at - (at > 4)


def slot_of(a, b, c):
    return (a * SIDE + b) * 2 + c


def kernel(
    nx, ny, emb, nbr, sid, live, cent, out, outc,
    embv, nbrv, sidv, centv, own, nb, cmat, zs, whi, wlo, cpad, e0, e2,
    f0, r0, f1, r1, f2, r2, f3, r3, s1, q1, s2, q2, s3, q3, s4, q4,
    load, halo_s, halo_r, ss, rs, seen,
):
    cells = own.shape[1] - 8 * BOUND
    dr = s2.shape[2]
    x, y = lax.axis_index("tx"), lax.axis_index("ty")
    core, chip = lax.rem(y, 2), y // 2
    chip_y, chip_x = chip // SIDE, lax.rem(chip, SIDE)
    pair = core * (SIDE * SIDE) + chip
    across = sorted(range(1, nx), key=lambda r: -min(r, nx - r))

    def on_tx(r):
        return (lax.rem(x + r, nx), y)

    def on_ty(a, b, c):
        to = lax.rem(chip_y + a, SIDE) * SIDE + lax.rem(chip_x + b, SIDE)
        return (x, to * 2 + lax.rem(core + c, 2))

    get_ids = pltpu.make_async_copy(nbr, nbrv, load.at[0])
    get_ids.start()
    get_emb = pltpu.make_async_copy(emb, embv, load.at[1])
    get_emb.start()
    get_sid = pltpu.make_async_copy(sid, sidv, load.at[2])
    get_sid.start()
    get_cent = pltpu.make_async_copy(cent, centv, load.at[3])
    get_cent.start()

    bar = pltpu.get_barrier_semaphore()

    def tile(a, b):
        return (lax.rem(x + a + nx, nx), lax.rem(y + b + ny, ny))

    def greet(sem, a, b):
        pl.semaphore_signal(sem, inc=1, device_id=tile(a, b), device_id_type=MESH)

    border = [(a, b) for a in (-1, 1) for b in (-1, 1)] + [(-1, 0), (1, 0), (0, -1), (0, 1)]
    first_met = border + [(a, 0) for a in (-4, -3, -2, 2, 3, 4)]
    for a, b in first_met:
        greet(bar, a, b)

    def greet_tx(step, d):
        for a in (-d, d):
            greet(seen.at[step], a, 0)

    def greet_ty(step, d):
        for b in (-d, d):
            greet(seen.at[step], 0, b)

    def heard(step):
        pl.semaphore_wait(seen.at[step], 2)

    r0[:, :, SLOTS:, :] = jnp.zeros((ITERS, nx, 8 - SLOTS, LANES), F32)
    r1[:, HALF:, :] = jnp.zeros((ITERS, PADDED - HALF, LANES), F32)
    r2[:, :, HALF:, :] = jnp.zeros((ITERS, SIDE * SIDE, PADDED - HALF, LANES), F32)
    r3[:, :, HALF:, :] = jnp.zeros((ITERS, 2, PADDED - HALF, LANES), F32)
    q1[:, :, SENT:, :] = jnp.zeros((ITERS, ny, CHUNK - SENT, LANES), F32)
    q4[:, PAIRS * BACK :, :] = jnp.zeros((ITERS, q4.shape[1] - PAIRS * BACK, LANES), F32)
    cpad[...] = jnp.zeros_like(cpad)
    own[PCS:, :cells] = jnp.zeros((ROWS - PCS, cells), F32)
    get_ids.wait()
    ids = nbrv[:, 0, 0, :]
    center = 5 * BOUND + cells - BOUND
    ids = jnp.where(ids < center, ids, jnp.where(ids < center + BOUND, ids - center, ids - BOUND))
    for n in range(ids.shape[0]):
        nb[n] = jnp.broadcast_to(ids[n : n + 1, :], (8, cells))
    rows8 = iota((8, cells), 0)

    def count(g, c):
        base = rows8 + g * 16
        low = jnp.zeros((8, cells), F32)
        high = jnp.zeros((8, cells), F32)
        for n in range(ids.shape[0]):
            here = nb[n]
            low = low + jnp.where(here == base, 1.0, 0.0)
            high = high + jnp.where(here == base + 8, 1.0, 0.0)
        at = pl.multiple_of(g * 16, 16)
        cmat[pl.ds(at, 16), :] = jnp.concatenate([low, high], axis=0).astype(BF16)
        return c

    groups = cmat.shape[0] // 16
    early = groups * 8 // 16
    lax.fori_loop(0, early, count, 0)
    get_emb.wait()
    own[:PCS, :cells] = embv[:, 0, 0, :]

    pl.semaphore_wait(bar, len(first_met))

    for a, b in border:
        pltpu.make_async_remote_copy(
            src_ref=own.at[:, pl.ds(0, BOUND)],
            dst_ref=own.at[:, pl.ds(cells + place_of(a, b) * BOUND, BOUND)],
            send_sem=halo_s,
            recv_sem=halo_r,
            device_id=tile(-a, -b),
            device_id_type=MESH,
        ).start()
    halo = pltpu.make_async_remote_copy(
        src_ref=own.at[:, pl.ds(cells, 8 * BOUND)],
        dst_ref=own.at[:, pl.ds(cells, 8 * BOUND)],
        send_sem=halo_s,
        recv_sem=halo_r,
        device_id=on_tx(1),
        device_id_type=MESH,
    )

    greet_tx(0, 4)
    greet_ty(1, 1)
    lax.fori_loop(early, groups, count, 0)

    alive = iota((1, cells), 1) < live[...]
    livef = alive.astype(F32)
    get_sid.wait()
    slides = sidv[0].astype(F32)
    left = jnp.where(alive, slides, 64.0)
    masks, names = [], []
    for _ in range(SLOTS):
        name = jnp.min(left, axis=1, keepdims=True)
        masks.append(jnp.where(left == name, livef, 0.0))
        names.append(jnp.where(name < 64.0, name, NONE))
        left = jnp.where(left > name, left, 64.0)
    row = iota((8, cells), 0)

    def stack(parts):
        total = jnp.zeros((8, cells), F32)
        for at, part in parts:
            total = total + jnp.where(row == at, part, 0.0)
        return total

    by_slot = list(enumerate(masks))
    mask8 = stack(by_slot)
    mask8_bf = mask8.astype(BF16)
    masked = stack(by_slot + [(SLOTS, 1.0 - livef)])
    masked2 = jnp.concatenate([masked, masked], axis=0).astype(BF16)
    slot_row = iota((8, LANES), 0)
    slot_lane = iota((8, LANES), 1)
    name8 = jnp.full((8, LANES), NONE, F32)
    for i in range(SLOTS):
        name8 = jnp.where(slot_row == i, dense_row(names[i]), name8)
    here8_bf = jnp.where(slot_lane.astype(F32) == name8, 1.0, 0.0)[:, : 2 * PADDED].astype(BF16)
    chunk_row = iota((CHUNK, LANES), 0)
    chunk_lane = iota((CHUNK, LANES), 1)
    chunk_name = jnp.zeros((CHUNK, LANES), F32)
    for first in (0, 5, 10):
        for i in range(SLOTS):
            chunk_name = jnp.where(chunk_row == first + i, names[i], chunk_name)
    chunk_name = jnp.where(chunk_lane == ID_LANE, chunk_name, 0.0)
    get_cent.wait()
    cpad[:PCS, :CLUSTERS] = centv[...]
    centre = cpad[...]

    heard(1)
    greet_ty(2, 2)
    halo.wait_recv()
    everything = own[...]
    part1 = everything.astype(BF16).astype(F32)
    rest = everything - part1
    part2 = rest.astype(BF16).astype(F32)
    parts = jnp.concatenate([part1, part2, rest - part2], axis=0).astype(BF16)
    summed = dot(parts, cmat[...], NN)
    summed = (summed[2 * ROWS :] + summed[ROWS : 2 * ROWS]) + summed[:ROWS]
    field = (everything[:, :cells] + summed) / (ids.shape[0] + 1.0)
    field = jnp.where(iota((ROWS, cells), 0) < PCS, field, 0.0) * livef

    heard(2)
    greet_ty(3, 4)
    heard(0)

    cluster = iota((LANES, cells), 0)
    lane40 = iota((1, LANES), 1)

    def sender(sem):
        def send(src, dst, to):
            pltpu.make_async_remote_copy(
                src_ref=src, dst_ref=dst, send_sem=ss.at[sem], recv_sem=rs.at[sem],
                device_id=to, device_id_type=MESH,
            ).start()

        return send

    def arrivals(sem, region):
        return pltpu.make_async_remote_copy(
            src_ref=region, dst_ref=region, send_sem=ss.at[sem], recv_sem=rs.at[sem],
            device_id=on_tx(1), device_id_type=MESH,
        )

    pending = []
    at_pairs = []
    for turn in range(ITERS):
        sem = turn * 8
        unit_y = centre * lax.rsqrt(jnp.sum(centre * centre, axis=0, keepdims=True) + 1.0)
        inverse = lax.rsqrt(jnp.sum(field * field, axis=0, keepdims=True) + 1.0)
        unit_z = field * inverse
        zs[...] = field
        yh, yl = parts_of(unit_y)
        zh, zl = parts_of(unit_z)
        score = dot(
            jnp.concatenate([yh, yh, yl, yl], axis=0).astype(BF16),
            jnp.concatenate([zh, zl, zh, zl], axis=0).astype(BF16),
            TN,
        )
        raw = jnp.where(cluster < CLUSTERS, jnp.exp(SHARPNESS * (score - 1.0)), 0.0)
        first = raw * (livef / jnp.sum(raw, axis=0, keepdims=True))
        first = jnp.where(cluster == LIVE_LANE, livef, first)
        occ = halves(dot(mask8_bf, jnp.concatenate(split2(first), axis=0), NT))
        occ = jnp.where(slot_lane == ID_LANE, name8, occ)

        f0[turn] = occ
        send = sender(sem)
        for r in across:
            send(f0.at[turn, pl.ds(0, SLOTS)], r0.at[turn, r, pl.ds(0, SLOTS)], on_tx(r))
        r0[turn, 0, :SLOTS] = occ[:SLOTS]

        if turn == 0:
            heard(3)
            greet_ty(4, 8)

        slots_a = stack(by_slot + [(4, inverse)] + [(5 + i, masks[i]) for i in range(3)])
        slots_b = stack([(0, masks[3]), (1, inverse)])
        ones_b = stack([(2 + i, masks[i]) for i in range(SLOTS)])

        def build(p, c):
            one = zs[pl.ds(p * 2, 1), :]
            two = zs[pl.ds(p * 2 + 1, 1), :]
            upper = jnp.where(row < 5, one, two) * slots_a
            lower = two * slots_b + ones_b
            hi, lo = split2(jnp.concatenate([upper, lower], axis=0))
            at = pl.multiple_of(p * CHUNK, CHUNK)
            whi[pl.ds(at, CHUNK), :] = hi
            wlo[pl.ds(at, CHUNK), :] = lo
            return c

        lax.fori_loop(0, PAIRS, build, 0)

        if turn == 0:
            heard(4)
        copy = arrivals(sem, r0.at[turn, pl.ds(1, nx - 1), pl.ds(0, SLOTS)])
        copy.wait_recv()
        pending.append(copy)
        got = r0[turn].reshape(nx * 8, LANES)
        if turn == 0:
            name = jnp.broadcast_to(got[:, ID_LANE : ID_LANE + 1], (nx * 8, LANES))
            lane = iota((nx * 8, LANES), 1).astype(F32)
            slot = lax.rem(iota((nx * 8, LANES), 0), 8)
            e0[...] = jnp.where((name == lane) & (slot < SLOTS), 1.0, 0.0).astype(BF16)
        part = halves(dot(e0[...], split_lanes(got), TN)[: 2 * PADDED])
        f1[turn] = part.reshape(2, PADDED, LANES)
        send = sender(sem + 1)
        send(f1.at[turn, 1 - core, pl.ds(0, HALF)], r1.at[turn, pl.ds(0, HALF)], on_ty(0, 0, 1))
        copy = arrivals(sem + 1, r1.at[turn, pl.ds(0, HALF)])
        copy.wait_recv()
        pending.append(copy)
        part = r1[turn] + f1[turn, core]
        f2[turn] = part
        send = sender(sem + 2)
        for a, b in SQUARE[:-1]:
            send(
                f2.at[turn, pl.ds(0, HALF)],
                r2.at[turn, a * SIDE + b, pl.ds(0, HALF)],
                on_ty(a, b, 0),
            )
        r2[turn, 0] = part
        copy = arrivals(sem + 2, r2.at[turn, pl.ds(1, SIDE * SIDE - 1), pl.ds(0, HALF)])
        copy.wait_recv()
        pending.append(copy)
        part = jnp.sum(r2[turn], axis=0)
        f3[turn] = part
        send = sender(sem + 7)
        send(f3.at[turn, pl.ds(0, HALF)], r3.at[turn, core, pl.ds(0, HALF)], on_ty(0, 0, 1))
        r3[turn, core] = part
        copy = arrivals(sem + 7, r3.at[turn, 0, pl.ds(0, HALF)])
        copy.wait_recv()
        pending.append(copy)
        occupied = r3[turn].reshape(2 * PADDED, LANES)
        totals = occupied[:, LIVE_LANE : LIVE_LANE + 1]
        expected = (
            jnp.sum(occupied, axis=0, keepdims=True)
            * totals
            / jnp.sum(totals, axis=0, keepdims=True)
        )
        ratio = (expected + 1.0) / (occupied + 1.0)
        ratio = jnp.where(lane40 < CLUSTERS, ratio * ratio, 1.0)
        mine = dot(here8_bf, split_lanes(ratio), NN)
        mine_hi = jnp.where(slot_row == SLOTS, 1.0, mine[:, :LANES])
        mine2 = jnp.concatenate([mine_hi, mine[:, LANES:]], axis=0).astype(BF16)
        weighted = raw * dot(mine2, masked2, TN)
        assign = weighted * (livef / jnp.sum(weighted, axis=0, keepdims=True))

        ah, al = split2(assign)
        both = jnp.concatenate([ah, al], axis=0)
        send = sender(sem + 3)
        chips = SIDE * SIDE
        for side, count_ in ((0, chips), (1, PAIRS - chips)):
            rows = pl.ds(side * chips * CHUNK, count_ * CHUNK)
            wide = dot(whi[rows, :], both, NT)
            sums = halves(wide) + dot(wlo[rows, :], ah, NT)
            sums = sums.reshape(count_, CHUNK, LANES) + chunk_name[None]
            s1[turn, pl.ds(side * chips, count_)] = sums
            c = lax.rem(core + side, 2)
            for a, b in SQUARE:
                to = lax.rem(chip_y + a, SIDE) * SIDE + lax.rem(chip_x + b, SIDE)

                def go(a=a, b=b, to=to, c=c, side=side):
                    send(
                        s1.at[turn, side * chips + to, pl.ds(0, SENT)],
                        q1.at[turn, (a * SIDE + b) * 2 + c, pl.ds(0, SENT)],
                        (x, to * 2 + side),
                    )

                if side == 0 and (a or b):
                    go()
                elif side == 0:
                    pl.when(core != side)(go)
                elif a or b:
                    pl.when(to < count_)(go)
                else:
                    pl.when((core != side) & (to < count_))(go)

        @pl.when(pair < PAIRS)
        def _():
            q1[turn, 0, :SENT] = s1[turn, pair, :SENT]
            arrivals(sem + 3, q1.at[turn, pl.ds(1, ny - 1), pl.ds(0, SENT)]).wait_recv()
            got = q1[turn].reshape(ny * CHUNK, LANES)
            if turn == 0:
                shape = (ny * CHUNK, LANES)
                at = lax.rem(iota(shape, 0), CHUNK)
                second = (at >= 5) & (at < 10)
                middle = (at == 4) | (at == 9)
                start = jnp.where(
                    middle,
                    3 * SLIDES + second.astype(jnp.int32),
                    jnp.where(second, SLIDES, jnp.where(at >= 10, 2 * SLIDES, 0)),
                ).astype(F32)
                name = jnp.broadcast_to(got[:, ID_LANE : ID_LANE + 1], shape)
                name = jnp.where(middle, 0.0, jnp.where(at < SENT, name, NONE))
                goal = start + name
                table = jnp.where(goal == iota(shape, 1).astype(F32), 1.0, 0.0)
                e2[...] = table.astype(BF16)
            part = halves(dot(e2[...], split_lanes(got), TN))
            s2[turn] = part.reshape(nx, dr, LANES)

            send = sender(sem + 4)
            for r in across:
                send(s2.at[turn, lax.rem(x + r, nx)], q2.at[turn, r], on_tx(r))
            q2[turn, 0] = s2[turn, x]
            arrivals(sem + 4, q2.at[turn, pl.ds(1, nx - 1)]).wait_recv()
            part = jnp.sum(q2[turn], axis=0)
            s3[turn] = part
            send = sender(sem + 5)
            for r in across:
                send(s3.at[turn], q3.at[turn, x], on_tx(r))
            q3[turn, x] = part
            arrivals(sem + 5, q3.at[turn, pl.ds(1, nx - 1)]).wait_recv()
            whole = q3[turn].reshape(nx * dr, LANES)
            counts = whole[2 * SLIDES : 3 * SLIDES]
            scale = 1.0 / (counts + 1.0)
            weight = jnp.sum(counts * scale, axis=0, keepdims=True)
            weight = jnp.where(lane40 < CLUSTERS, weight, 1.0)
            betas = []
            for j in range(2):
                part = whole[j * SLIDES : (j + 1) * SLIDES]
                mean = jnp.sum(part * scale, axis=0, keepdims=True) / weight
                betas.append((part - counts * mean) * scale)
            betas.append(whole[2 * SLIDES :])
            chosen = halves(dot(e2[...], split_lanes(jnp.concatenate(betas, axis=0)), NN))
            s4[turn] = chosen.reshape(ny, CHUNK, LANES)

            send = sender(sem + 6)
            for a, b, c in OTHERS:
                send(
                    s4.at[turn, slot_of(a, b, c), pl.ds(0, BACK)],
                    q4.at[turn, pl.ds(pair * BACK, BACK)],
                    on_ty(SIDE - a, SIDE - b, 2 - c),
                )
            q4[turn, pl.ds(pair * BACK, BACK)] = s4[turn, 0, :BACK]
            arrivals(sem + 6, q4.at[turn, pl.ds(0, (PAIRS - 1) * BACK)]).wait_recv()

        @pl.when(pair >= PAIRS)
        def _():
            arrivals(sem + 6, q4.at[turn, pl.ds(0, PAIRS * BACK)]).wait_recv()

        slot_beta = [q4[turn, pl.ds(i, ROWS, stride=5), :] for i in range(SLOTS)]
        bh, bl = split2(jnp.concatenate(slot_beta, axis=0))
        shifts = dot(jnp.concatenate([bh, bh], axis=1), both, NN) + dot(bl, ah, NN)
        for i in range(SLOTS):
            field = field - shifts[i * ROWS : (i + 1) * ROWS] * masks[i]
        centre = q4[turn, pl.ds(SLOTS, ROWS, stride=5), :]

    out[:, 0, 0, :] = field[:PCS]
    unit_y = centre / jnp.sqrt(jnp.sum(centre * centre, axis=0, keepdims=True) + 1.0)
    outc[...] = unit_y[:PCS, :CLUSTERS]

    halo.wait_send()
    for copy in pending:
        copy.wait_send()
    for turn in range(ITERS):
        sem = turn * 8

        @pl.when(pair < PAIRS)
        def _():
            arrivals(sem + 3, q1.at[turn, pl.ds(0, PAIRS - 1), pl.ds(0, SENT)]).wait_send()
            arrivals(sem + 4, q2.at[turn, pl.ds(1, nx - 1)]).wait_send()
            arrivals(sem + 5, q3.at[turn, pl.ds(1, nx - 1)]).wait_send()
            arrivals(sem + 6, s4.at[turn, pl.ds(1, ny - 1), pl.ds(0, BACK)]).wait_send()

        @pl.when(pair >= PAIRS)
        def _():
            arrivals(sem + 3, q1.at[turn, pl.ds(0, PAIRS), pl.ds(0, SENT)]).wait_send()


def hand_over(a, b, c, d, sems):
    copies = [
        pltpu.make_async_copy(a, c, sems.at[0]),
        pltpu.make_async_copy(b, d, sems.at[1]),
    ]
    for copy in copies:
        copy.start()
    for copy in copies:
        copy.wait()


def per_device(nx, ny, embedding, neighbors, slide_id, live_count, centroids):
    cells = embedding.shape[3]
    near = neighbors.shape[0]
    dr = -(-DENSE // (nx * 8)) * 8
    vmem = pl.BlockSpec(memory_space=pltpu.VMEM)
    hbm = pl.BlockSpec(memory_space=pltpu.HBM)

    def far(v):
        return pltpu.with_memory_space_constraint(v, pltpu.HBM)

    def buf(*shape):
        return pltpu.VMEM((ITERS,) + shape, F32)

    corrected, centers = pl.pallas_call(
        functools.partial(kernel, nx, ny),
        out_shape=(
            jax.ShapeDtypeStruct(embedding.shape, F32),
            jax.ShapeDtypeStruct((PCS, CLUSTERS), F32),
        ),
        in_specs=[hbm, hbm, hbm, vmem, hbm],
        out_specs=(vmem, vmem),
        scratch_shapes=[
            pltpu.VMEM(embedding.shape, F32),
            pltpu.VMEM(neighbors.shape, jnp.int32),
            pltpu.VMEM(slide_id.shape, jnp.int32),
            pltpu.VMEM((PCS, CLUSTERS), F32),
            pltpu.VMEM((ROWS, cells + 8 * BOUND), F32),
            pltpu.VMEM((near, 8, cells), jnp.int32),
            pltpu.VMEM((cells + 8 * BOUND, cells), BF16),
            pltpu.VMEM((ROWS, cells), F32),
            pltpu.VMEM((PAIRS * CHUNK, cells), BF16),
            pltpu.VMEM((PAIRS * CHUNK, cells), BF16),
            pltpu.VMEM((ROWS, LANES), F32),
            pltpu.VMEM((nx * 8, LANES), BF16),
            pltpu.VMEM((ny * CHUNK, LANES), BF16),
            buf(8, LANES),
            buf(nx, 8, LANES),
            buf(2, PADDED, LANES),
            buf(PADDED, LANES),
            buf(PADDED, LANES),
            buf(SIDE * SIDE, PADDED, LANES),
            buf(PADDED, LANES),
            buf(2, PADDED, LANES),
            buf(PAIRS, CHUNK, LANES),
            buf(ny, CHUNK, LANES),
            buf(nx, dr, LANES),
            buf(nx, dr, LANES),
            buf(dr, LANES),
            buf(nx, dr, LANES),
            buf(ny, CHUNK, LANES),
            buf(ROWS * 5 + 8, LANES),
            pltpu.SemaphoreType.DMA((4,)),
            pltpu.SemaphoreType.DMA,
            pltpu.SemaphoreType.DMA,
            pltpu.SemaphoreType.DMA((8 * ITERS,)),
            pltpu.SemaphoreType.DMA((8 * ITERS,)),
            pltpu.SemaphoreType.REGULAR((5,)),
        ],
        compiler_params=pltpu.CompilerParams(
            collective_id=0, has_side_effects=True, vmem_limit_bytes=48 * 1024 * 1024
        ),
        name="harmony",
    )(far(embedding), far(neighbors), far(slide_id), live_count, far(centroids.T))
    corrected, centers = pl.pallas_call(
        hand_over,
        out_shape=(
            jax.ShapeDtypeStruct(embedding.shape, F32),
            jax.ShapeDtypeStruct((PCS, CLUSTERS), F32),
        ),
        in_specs=[vmem] * 2,
        out_specs=(hbm, hbm),
        scratch_shapes=[pltpu.SemaphoreType.DMA((2,))],
        name="handover",
    )(
        pltpu.with_memory_space_constraint(corrected, pltpu.VMEM),
        pltpu.with_memory_space_constraint(centers, pltpu.VMEM),
    )
    return corrected, centers.T


def solution(mesh):
    nx, ny = mesh.shape["tx"], mesh.shape["ty"]
    placed = (
        P(None, "tx", "ty", None),
        P(None, "tx", "ty", None),
        P("tx", "ty", None),
        P("tx", "ty"),
        P(),
    )
    return jax.shard_map(
        functools.partial(per_device, nx, ny),
        mesh=mesh,
        in_specs=placed,
        out_specs=(P(None, "tx", "ty", None), P()),
        check_vma=False,
    )
```

```python
import functools

import jax
import jax.numpy as jnp
from jax import lax
from jax.experimental import pallas as pl
from jax.experimental.pallas import tpu as pltpu
from jax.sharding import PartitionSpec as P

SLIDES = 40
SLOTS = 4
ITERS = 2
CLUSTERS = 100
PCS = 50
BOUND = 128
SHARPNESS = 20.0

LANES = 128
ROWS = 56
PAIRS = 25
CHUNK = 16
SENT = 14
BACK = 10
HALF = 20
PADDED = 24
ID_LANE = 126
LIVE_LANE = 127
NONE = -1000.0

F32 = jnp.float32
BF16 = jnp.bfloat16
MESH = pl.DeviceIdType.MESH

NN = (((1,), (0,)), ((), ()))
NT = (((1,), (1,)), ((), ()))
TN = (((0,), (0,)), ((), ()))


def dot(a, b, dims):
    return lax.dot_general(a, b, dims, preferred_element_type=F32)


def split2(v):
    hi = v.astype(BF16)
    return hi, (v - hi.astype(F32)).astype(BF16)


def halves(v):
    return v[:, :LANES] + v[:, LANES:]


def split_lanes(v):
    return jnp.concatenate(split2(v), axis=1)


def parts_of(v):
    hi = v.astype(BF16).astype(F32)
    return hi, v - hi


def iota(shape, dim):
    return lax.broadcasted_iota(jnp.int32, shape, dim)


SIDE = 4


def ring(a):
    return min(a, SIDE - a)


SQUARE = sorted(
    ((a, b) for a in range(SIDE) for b in range(SIDE)), key=lambda o: -ring(o[0]) - ring(o[1])
)
OTHERS = [(a, b, c) for a, b in SQUARE for c in (1, 0) if a or b or c]
NEAR = [(0, b, c) for b in (2, 1, 3, 0) for c in (1, 0) if b or c]
FAR = [(a, 0, 0) for a in (2, 1, 3)]
DENSE = 3 * SLIDES + 2


def dense_row(name):
    return jnp.where(name >= HALF, name + (PADDED - HALF), name)


def place_of(a, b):
    at = (a + 1) * 3 + b + 1
    return at - (at > 4)


def slot_of(a, b, c):
    return (a * SIDE + b) * 2 + c


def kernel(
    nx, ny, emb, nbr, sid, live, cent, out, outc,
    embv, nbrv, sidv, centv, own, nb, cmat, zs, whi, wlo, cpad, e0, e2,
    f0, r0, f2, r2, f3, r3, s1, q1, s2, q2, s3, q3, s4, q4,
    load, halo_s, halo_r, ss, rs, seen,
):
    cells = own.shape[1] - 8 * BOUND
    dr = s2.shape[2]
    x, y = lax.axis_index("tx"), lax.axis_index("ty")
    core, chip = lax.rem(y, 2), y // 2
    chip_y, chip_x = chip // SIDE, lax.rem(chip, SIDE)
    pair = core * (SIDE * SIDE) + chip
    across = sorted(range(1, nx), key=lambda r: -min(r, nx - r))

    def on_tx(r):
        return (lax.rem(x + r, nx), y)

    def on_ty(a, b, c):
        to = lax.rem(chip_y + a, SIDE) * SIDE + lax.rem(chip_x + b, SIDE)
        return (x, to * 2 + lax.rem(core + c, 2))

    get_ids = pltpu.make_async_copy(nbr, nbrv, load.at[0])
    get_ids.start()
    get_emb = pltpu.make_async_copy(emb, embv, load.at[1])
    get_emb.start()
    get_sid = pltpu.make_async_copy(sid, sidv, load.at[2])
    get_sid.start()
    get_cent = pltpu.make_async_copy(cent, centv, load.at[3])
    get_cent.start()

    bar = pltpu.get_barrier_semaphore()

    def tile(a, b):
        return (lax.rem(x + a + nx, nx), lax.rem(y + b + ny, ny))

    def greet(sem, a, b):
        pl.semaphore_signal(sem, inc=1, device_id=tile(a, b), device_id_type=MESH)

    border = [(a, b) for a in (-1, 1) for b in (-1, 1)] + [(-1, 0), (1, 0), (0, -1), (0, 1)]
    other = 1 - 2 * core
    first_met = border + [(a, b) for a in (-4, -3, -2, 2, 3, 4) for b in (0, other)]
    for a, b in first_met:
        greet(bar, a, b)

    def greet_tx(step, d):
        for a in (-d, d):
            greet(seen.at[step], a, 0)

    def greet_ty(step, d):
        for b in (-d, d):
            greet(seen.at[step], 0, b)

    def heard(step):
        pl.semaphore_wait(seen.at[step], 2)

    r0[:, :, SLOTS:, :] = jnp.zeros((ITERS, 2 * nx, 8 - SLOTS, LANES), F32)
    r2[:, :, HALF:, :] = jnp.zeros((ITERS, SIDE * SIDE, PADDED - HALF, LANES), F32)
    r3[:, :, HALF:, :] = jnp.zeros((ITERS, 2, PADDED - HALF, LANES), F32)
    q1[:, :, SENT:, :] = jnp.zeros((ITERS, ny, CHUNK - SENT, LANES), F32)
    q4[:, PAIRS * BACK :, :] = jnp.zeros((ITERS, q4.shape[1] - PAIRS * BACK, LANES), F32)
    cpad[...] = jnp.zeros_like(cpad)
    own[PCS:, :cells] = jnp.zeros((ROWS - PCS, cells), F32)
    get_ids.wait()
    ids = nbrv[:, 0, 0, :]
    center = 5 * BOUND + cells - BOUND
    ids = jnp.where(ids < center, ids, jnp.where(ids < center + BOUND, ids - center, ids - BOUND))
    for n in range(ids.shape[0]):
        nb[n] = jnp.broadcast_to(ids[n : n + 1, :], (8, cells))
    rows8 = iota((8, cells), 0)

    def count(g, c):
        base = rows8 + g * 16
        low = jnp.zeros((8, cells), F32)
        high = jnp.zeros((8, cells), F32)
        for n in range(ids.shape[0]):
            here = nb[n]
            low = low + jnp.where(here == base, 1.0, 0.0)
            high = high + jnp.where(here == base + 8, 1.0, 0.0)
        at = pl.multiple_of(g * 16, 16)
        cmat[pl.ds(at, 16), :] = jnp.concatenate([low, high], axis=0).astype(BF16)
        return c

    groups = cmat.shape[0] // 16
    early = groups * 8 // 16
    lax.fori_loop(0, early, count, 0)
    get_emb.wait()
    own[:PCS, :cells] = embv[:, 0, 0, :]

    pl.semaphore_wait(bar, len(first_met))

    for a, b in border:
        pltpu.make_async_remote_copy(
            src_ref=own.at[:, pl.ds(0, BOUND)],
            dst_ref=own.at[:, pl.ds(cells + place_of(a, b) * BOUND, BOUND)],
            send_sem=halo_s,
            recv_sem=halo_r,
            device_id=tile(-a, -b),
            device_id_type=MESH,
        ).start()
    halo = pltpu.make_async_remote_copy(
        src_ref=own.at[:, pl.ds(cells, 8 * BOUND)],
        dst_ref=own.at[:, pl.ds(cells, 8 * BOUND)],
        send_sem=halo_s,
        recv_sem=halo_r,
        device_id=on_tx(1),
        device_id_type=MESH,
    )

    greet_tx(0, 4)
    greet_ty(1, 1)
    lax.fori_loop(early, groups, count, 0)

    alive = iota((1, cells), 1) < live[...]
    livef = alive.astype(F32)
    get_sid.wait()
    slides = sidv[0].astype(F32)
    left = jnp.where(alive, slides, 64.0)
    masks, names = [], []
    for _ in range(SLOTS):
        name = jnp.min(left, axis=1, keepdims=True)
        masks.append(jnp.where(left == name, livef, 0.0))
        names.append(jnp.where(name < 64.0, name, NONE))
        left = jnp.where(left > name, left, 64.0)
    row = iota((8, cells), 0)

    def stack(parts):
        total = jnp.zeros((8, cells), F32)
        for at, part in parts:
            total = total + jnp.where(row == at, part, 0.0)
        return total

    by_slot = list(enumerate(masks))
    mask8 = stack(by_slot)
    mask8_bf = mask8.astype(BF16)
    masked = stack(by_slot + [(SLOTS, 1.0 - livef)])
    masked2 = jnp.concatenate([masked, masked], axis=0).astype(BF16)
    slot_row = iota((8, LANES), 0)
    slot_lane = iota((8, LANES), 1)
    name8 = jnp.full((8, LANES), NONE, F32)
    for i in range(SLOTS):
        name8 = jnp.where(slot_row == i, dense_row(names[i]), name8)
    here8_bf = jnp.where(slot_lane.astype(F32) == name8, 1.0, 0.0)[:, : 2 * PADDED].astype(BF16)
    chunk_row = iota((CHUNK, LANES), 0)
    chunk_lane = iota((CHUNK, LANES), 1)
    chunk_name = jnp.zeros((CHUNK, LANES), F32)
    for first in (0, 5, 10):
        for i in range(SLOTS):
            chunk_name = jnp.where(chunk_row == first + i, names[i], chunk_name)
    chunk_name = jnp.where(chunk_lane == ID_LANE, chunk_name, 0.0)
    get_cent.wait()
    cpad[:PCS, :CLUSTERS] = centv[...]
    centre = cpad[...]

    heard(1)
    greet_ty(2, 2)
    halo.wait_recv()
    everything = own[...]
    part1 = everything.astype(BF16).astype(F32)
    rest = everything - part1
    part2 = rest.astype(BF16).astype(F32)
    parts = jnp.concatenate([part1, part2, rest - part2], axis=0).astype(BF16)
    summed = dot(parts, cmat[...], NN)
    summed = (summed[2 * ROWS :] + summed[ROWS : 2 * ROWS]) + summed[:ROWS]
    field = (everything[:, :cells] + summed) / (ids.shape[0] + 1.0)
    field = jnp.where(iota((ROWS, cells), 0) < PCS, field, 0.0) * livef

    heard(2)
    greet_ty(3, 4)
    heard(0)

    cluster = iota((LANES, cells), 0)
    lane40 = iota((1, LANES), 1)

    def sender(sem):
        def send(src, dst, to):
            pltpu.make_async_remote_copy(
                src_ref=src, dst_ref=dst, send_sem=ss.at[sem], recv_sem=rs.at[sem],
                device_id=to, device_id_type=MESH,
            ).start()

        return send

    def arrivals(sem, region):
        return pltpu.make_async_remote_copy(
            src_ref=region, dst_ref=region, send_sem=ss.at[sem], recv_sem=rs.at[sem],
            device_id=on_tx(1), device_id_type=MESH,
        )

    pending = []
    at_pairs = []
    for turn in range(ITERS):
        sem = turn * 8
        unit_y = centre * lax.rsqrt(jnp.sum(centre * centre, axis=0, keepdims=True) + 1.0)
        inverse = lax.rsqrt(jnp.sum(field * field, axis=0, keepdims=True) + 1.0)
        unit_z = field * inverse
        zs[...] = field
        yh, yl = parts_of(unit_y)
        zh, zl = parts_of(unit_z)
        score = dot(
            jnp.concatenate([yh, yh, yl, yl], axis=0).astype(BF16),
            jnp.concatenate([zh, zl, zh, zl], axis=0).astype(BF16),
            TN,
        )
        raw = jnp.where(cluster < CLUSTERS, jnp.exp(SHARPNESS * (score - 1.0)), 0.0)
        first = raw * (livef / jnp.sum(raw, axis=0, keepdims=True))
        first = jnp.where(cluster == LIVE_LANE, livef, first)
        occ = halves(dot(mask8_bf, jnp.concatenate(split2(first), axis=0), NT))
        occ = jnp.where(slot_lane == ID_LANE, name8, occ)

        f0[turn] = occ
        send = sender(sem)
        for r in across + [0]:
            for c in (1, 0):
                if r or c:
                    send(
                        f0.at[turn, pl.ds(0, SLOTS)],
                        r0.at[turn, r * 2 + c, pl.ds(0, SLOTS)],
                        (lax.rem(x + r, nx), chip * 2 + lax.rem(core + c, 2)),
                    )
        r0[turn, 0, :SLOTS] = occ[:SLOTS]

        if turn == 0:
            heard(3)
            greet_ty(4, 8)

        slots_a = stack(by_slot + [(4, inverse)] + [(5 + i, masks[i]) for i in range(3)])
        slots_b = stack([(0, masks[3]), (1, inverse)])
        ones_b = stack([(2 + i, masks[i]) for i in range(SLOTS)])

        def build(p, c):
            one = zs[pl.ds(p * 2, 1), :]
            two = zs[pl.ds(p * 2 + 1, 1), :]
            upper = jnp.where(row < 5, one, two) * slots_a
            lower = two * slots_b + ones_b
            hi, lo = split2(jnp.concatenate([upper, lower], axis=0))
            at = pl.multiple_of(p * CHUNK, CHUNK)
            whi[pl.ds(at, CHUNK), :] = hi
            wlo[pl.ds(at, CHUNK), :] = lo
            return c

        lax.fori_loop(0, PAIRS, build, 0)

        if turn == 0:
            heard(4)
        copy = arrivals(sem, r0.at[turn, pl.ds(1, 2 * nx - 1), pl.ds(0, SLOTS)])
        copy.wait_recv()
        pending.append(copy)
        got = r0[turn].reshape(2 * nx * 8, LANES)
        if turn == 0:
            name = jnp.broadcast_to(got[:, ID_LANE : ID_LANE + 1], got.shape)
            half_row = (iota(got.shape, 1) + core * PADDED).astype(F32)
            slot = lax.rem(iota(got.shape, 0), 8)
            e0[...] = jnp.where((name == half_row) & (slot < SLOTS), 1.0, 0.0).astype(BF16)
        part = halves(dot(e0[...], split_lanes(got), TN)[:PADDED])
        f2[turn] = part
        send = sender(sem + 2)
        for a, b in SQUARE[:-1]:
            send(
                f2.at[turn, pl.ds(0, HALF)],
                r2.at[turn, a * SIDE + b, pl.ds(0, HALF)],
                on_ty(a, b, 0),
            )
        r2[turn, 0] = part
        copy = arrivals(sem + 2, r2.at[turn, pl.ds(1, SIDE * SIDE - 1), pl.ds(0, HALF)])
        copy.wait_recv()
        pending.append(copy)
        part = jnp.sum(r2[turn], axis=0)
        f3[turn] = part
        send = sender(sem + 7)
        send(f3.at[turn, pl.ds(0, HALF)], r3.at[turn, core, pl.ds(0, HALF)], on_ty(0, 0, 1))
        r3[turn, core] = part
        copy = arrivals(sem + 7, r3.at[turn, 0, pl.ds(0, HALF)])
        copy.wait_recv()
        pending.append(copy)
        occupied = r3[turn].reshape(2 * PADDED, LANES)
        totals = occupied[:, LIVE_LANE : LIVE_LANE + 1]
        expected = (
            jnp.sum(occupied, axis=0, keepdims=True)
            * totals
            / jnp.sum(totals, axis=0, keepdims=True)
        )
        ratio = (expected + 1.0) / (occupied + 1.0)
        ratio = jnp.where(lane40 < CLUSTERS, ratio * ratio, 1.0)
        mine = dot(here8_bf, split_lanes(ratio), NN)
        mine_hi = jnp.where(slot_row == SLOTS, 1.0, mine[:, :LANES])
        mine2 = jnp.concatenate([mine_hi, mine[:, LANES:]], axis=0).astype(BF16)
        weighted = raw * dot(mine2, masked2, TN)
        assign = weighted * (livef / jnp.sum(weighted, axis=0, keepdims=True))

        ah, al = split2(assign)
        both = jnp.concatenate([ah, al], axis=0)
        send = sender(sem + 3)
        chips = SIDE * SIDE
        for side, count_ in ((0, chips), (1, PAIRS - chips)):
            rows = pl.ds(side * chips * CHUNK, count_ * CHUNK)
            wide = dot(whi[rows, :], both, NT)
            sums = halves(wide) + dot(wlo[rows, :], ah, NT)
            sums = sums.reshape(count_, CHUNK, LANES) + chunk_name[None]
            s1[turn, pl.ds(side * chips, count_)] = sums
            c = lax.rem(core + side, 2)
            for a, b in SQUARE:
                to = lax.rem(chip_y + a, SIDE) * SIDE + lax.rem(chip_x + b, SIDE)

                def go(a=a, b=b, to=to, c=c, side=side):
                    send(
                        s1.at[turn, side * chips + to, pl.ds(0, SENT)],
                        q1.at[turn, (a * SIDE + b) * 2 + c, pl.ds(0, SENT)],
                        (x, to * 2 + side),
                    )

                if side == 0 and (a or b):
                    go()
                elif side == 0:
                    pl.when(core != side)(go)
                elif a or b:
                    pl.when(to < count_)(go)
                else:
                    pl.when((core != side) & (to < count_))(go)

        @pl.when(pair < PAIRS)
        def _():
            q1[turn, 0, :SENT] = s1[turn, pair, :SENT]
            arrivals(sem + 3, q1.at[turn, pl.ds(1, ny - 1), pl.ds(0, SENT)]).wait_recv()
            got = q1[turn].reshape(ny * CHUNK, LANES)
            if turn == 0:
                shape = (ny * CHUNK, LANES)
                at = lax.rem(iota(shape, 0), CHUNK)
                second = (at >= 5) & (at < 10)
                middle = (at == 4) | (at == 9)
                start = jnp.where(
                    middle,
                    3 * SLIDES + second.astype(jnp.int32),
                    jnp.where(second, SLIDES, jnp.where(at >= 10, 2 * SLIDES, 0)),
                ).astype(F32)
                name = jnp.broadcast_to(got[:, ID_LANE : ID_LANE + 1], shape)
                name = jnp.where(middle, 0.0, jnp.where(at < SENT, name, NONE))
                goal = start + name
                table = jnp.where(goal == iota(shape, 1).astype(F32), 1.0, 0.0)
                e2[...] = table.astype(BF16)
            part = halves(dot(e2[...], split_lanes(got), TN))
            s2[turn] = part.reshape(nx, dr, LANES)

            send = sender(sem + 4)
            for r in across:
                send(s2.at[turn, lax.rem(x + r, nx)], q2.at[turn, r], on_tx(r))
            q2[turn, 0] = s2[turn, x]
            arrivals(sem + 4, q2.at[turn, pl.ds(1, nx - 1)]).wait_recv()
            part = jnp.sum(q2[turn], axis=0)
            s3[turn] = part
            send = sender(sem + 5)
            for r in across:
                send(s3.at[turn], q3.at[turn, x], on_tx(r))
            q3[turn, x] = part
            arrivals(sem + 5, q3.at[turn, pl.ds(1, nx - 1)]).wait_recv()
            whole = q3[turn].reshape(nx * dr, LANES)
            counts = whole[2 * SLIDES : 3 * SLIDES]
            scale = 1.0 / (counts + 1.0)
            weight = jnp.sum(counts * scale, axis=0, keepdims=True)
            weight = jnp.where(lane40 < CLUSTERS, weight, 1.0)
            betas = []
            for j in range(2):
                part = whole[j * SLIDES : (j + 1) * SLIDES]
                mean = jnp.sum(part * scale, axis=0, keepdims=True) / weight
                betas.append((part - counts * mean) * scale)
            betas.append(whole[2 * SLIDES :])
            betas = split_lanes(jnp.concatenate(betas, axis=0))

            send = sender(sem + 6)
            group = 2 * SIDE
            for a in (2, 1, 3, 0):
                rows = pl.ds(a * group * CHUNK, group * CHUNK)
                chosen = halves(dot(e2[rows, :], betas, NN))
                s4[turn, pl.ds(a * group, group)] = chosen.reshape(group, CHUNK, LANES)
                for b in (2, 1, 3, 0):
                    for c in (1, 0):
                        if a or b or c:
                            send(
                                s4.at[turn, slot_of(a, b, c), pl.ds(0, BACK)],
                                q4.at[turn, pl.ds(pair * BACK, BACK)],
                                on_ty(SIDE - a, SIDE - b, 2 - c),
                            )
            q4[turn, pl.ds(pair * BACK, BACK)] = s4[turn, 0, :BACK]
            arrivals(sem + 6, q4.at[turn, pl.ds(0, (PAIRS - 1) * BACK)]).wait_recv()

        @pl.when(pair >= PAIRS)
        def _():
            arrivals(sem + 6, q4.at[turn, pl.ds(0, PAIRS * BACK)]).wait_recv()

        slot_beta = [q4[turn, pl.ds(i, ROWS, stride=5), :] for i in range(SLOTS)]
        bh, bl = split2(jnp.concatenate(slot_beta, axis=0))
        shifts = dot(jnp.concatenate([bh, bh], axis=1), both, NN) + dot(bl, ah, NN)
        for i in range(SLOTS):
            field = field - shifts[i * ROWS : (i + 1) * ROWS] * masks[i]
        centre = q4[turn, pl.ds(SLOTS, ROWS, stride=5), :]

    out[:, 0, 0, :] = field[:PCS]
    unit_y = centre / jnp.sqrt(jnp.sum(centre * centre, axis=0, keepdims=True) + 1.0)
    outc[...] = unit_y[:PCS, :CLUSTERS]

    halo.wait_send()
    for copy in pending:
        copy.wait_send()
    for turn in range(ITERS):
        sem = turn * 8

        @pl.when(pair < PAIRS)
        def _():
            arrivals(sem + 3, q1.at[turn, pl.ds(0, PAIRS - 1), pl.ds(0, SENT)]).wait_send()
            arrivals(sem + 4, q2.at[turn, pl.ds(1, nx - 1)]).wait_send()
            arrivals(sem + 5, q3.at[turn, pl.ds(1, nx - 1)]).wait_send()
            arrivals(sem + 6, s4.at[turn, pl.ds(1, ny - 1), pl.ds(0, BACK)]).wait_send()

        @pl.when(pair >= PAIRS)
        def _():
            arrivals(sem + 3, q1.at[turn, pl.ds(0, PAIRS), pl.ds(0, SENT)]).wait_send()


def hand_over(a, b, c, d, sems):
    copies = [
        pltpu.make_async_copy(a, c, sems.at[0]),
        pltpu.make_async_copy(b, d, sems.at[1]),
    ]
    for copy in copies:
        copy.start()
    for copy in copies:
        copy.wait()


def per_device(nx, ny, embedding, neighbors, slide_id, live_count, centroids):
    cells = embedding.shape[3]
    near = neighbors.shape[0]
    dr = -(-DENSE // (nx * 8)) * 8
    vmem = pl.BlockSpec(memory_space=pltpu.VMEM)
    hbm = pl.BlockSpec(memory_space=pltpu.HBM)

    def far(v):
        return pltpu.with_memory_space_constraint(v, pltpu.HBM)

    def buf(*shape):
        return pltpu.VMEM((ITERS,) + shape, F32)

    corrected, centers = pl.pallas_call(
        functools.partial(kernel, nx, ny),
        out_shape=(
            jax.ShapeDtypeStruct(embedding.shape, F32),
            jax.ShapeDtypeStruct((PCS, CLUSTERS), F32),
        ),
        in_specs=[hbm, hbm, hbm, vmem, hbm],
        out_specs=(vmem, vmem),
        scratch_shapes=[
            pltpu.VMEM(embedding.shape, F32),
            pltpu.VMEM(neighbors.shape, jnp.int32),
            pltpu.VMEM(slide_id.shape, jnp.int32),
            pltpu.VMEM((PCS, CLUSTERS), F32),
            pltpu.VMEM((ROWS, cells + 8 * BOUND), F32),
            pltpu.VMEM((near, 8, cells), jnp.int32),
            pltpu.VMEM((cells + 8 * BOUND, cells), BF16),
            pltpu.VMEM((ROWS, cells), F32),
            pltpu.VMEM((PAIRS * CHUNK, cells), BF16),
            pltpu.VMEM((PAIRS * CHUNK, cells), BF16),
            pltpu.VMEM((ROWS, LANES), F32),
            pltpu.VMEM((2 * nx * 8, LANES), BF16),
            pltpu.VMEM((ny * CHUNK, LANES), BF16),
            buf(8, LANES),
            buf(2 * nx, 8, LANES),
            buf(PADDED, LANES),
            buf(SIDE * SIDE, PADDED, LANES),
            buf(PADDED, LANES),
            buf(2, PADDED, LANES),
            buf(PAIRS, CHUNK, LANES),
            buf(ny, CHUNK, LANES),
            buf(nx, dr, LANES),
            buf(nx, dr, LANES),
            buf(dr, LANES),
            buf(nx, dr, LANES),
            buf(ny, CHUNK, LANES),
            buf(ROWS * 5 + 8, LANES),
            pltpu.SemaphoreType.DMA((4,)),
            pltpu.SemaphoreType.DMA,
            pltpu.SemaphoreType.DMA,
            pltpu.SemaphoreType.DMA((8 * ITERS,)),
            pltpu.SemaphoreType.DMA((8 * ITERS,)),
            pltpu.SemaphoreType.REGULAR((5,)),
        ],
        compiler_params=pltpu.CompilerParams(
            collective_id=0, has_side_effects=True, vmem_limit_bytes=48 * 1024 * 1024
        ),
        name="harmony",
    )(far(embedding), far(neighbors), far(slide_id), live_count, far(centroids.T))
    corrected, centers = pl.pallas_call(
        hand_over,
        out_shape=(
            jax.ShapeDtypeStruct(embedding.shape, F32),
            jax.ShapeDtypeStruct((PCS, CLUSTERS), F32),
        ),
        in_specs=[vmem] * 2,
        out_specs=(hbm, hbm),
        scratch_shapes=[pltpu.SemaphoreType.DMA((2,))],
        name="handover",
    )(
        pltpu.with_memory_space_constraint(corrected, pltpu.VMEM),
        pltpu.with_memory_space_constraint(centers, pltpu.VMEM),
    )
    return corrected, centers.T


def solution(mesh):
    nx, ny = mesh.shape["tx"], mesh.shape["ty"]
    placed = (
        P(None, "tx", "ty", None),
        P(None, "tx", "ty", None),
        P("tx", "ty", None),
        P("tx", "ty"),
        P(),
    )
    return jax.shard_map(
        functools.partial(per_device, nx, ny),
        mesh=mesh,
        in_specs=placed,
        out_specs=(P(None, "tx", "ty", None), P()),
        check_vma=False,
    )
```

```python
import functools

import jax
import jax.numpy as jnp
from jax import lax
from jax.experimental import pallas as pl
from jax.experimental.pallas import tpu as pltpu
from jax.sharding import PartitionSpec as P

SLIDES = 40
SLOTS = 4
ITERS = 2
CLUSTERS = 100
PCS = 50
BOUND = 128
SHARPNESS = 20.0

LANES = 128
ROWS = 56
PAIRS = 25
CHUNK = 16
SENT = 14
BACK = 10
HALF = 20
PADDED = 24
ID_LANE = 126
LIVE_LANE = 127
NONE = -1000.0

F32 = jnp.float32
BF16 = jnp.bfloat16
MESH = pl.DeviceIdType.MESH

NN = (((1,), (0,)), ((), ()))
NT = (((1,), (1,)), ((), ()))
TN = (((0,), (0,)), ((), ()))


def dot(a, b, dims):
    return lax.dot_general(a, b, dims, preferred_element_type=F32)


def split2(v):
    hi = v.astype(BF16)
    return hi, (v - hi.astype(F32)).astype(BF16)


def halves(v):
    return v[:, :LANES] + v[:, LANES:]


def split_lanes(v):
    return jnp.concatenate(split2(v), axis=1)


def parts_of(v):
    hi = v.astype(BF16).astype(F32)
    return hi, v - hi


def iota(shape, dim):
    return lax.broadcasted_iota(jnp.int32, shape, dim)


SIDE = 4


def ring(a):
    return min(a, SIDE - a)


SQUARE = sorted(
    ((a, b) for a in range(SIDE) for b in range(SIDE)), key=lambda o: -ring(o[0]) - ring(o[1])
)
OTHERS = [(a, b, c) for a, b in SQUARE for c in (1, 0) if a or b or c]
NEAR = [(0, b, c) for b in (2, 1, 3, 0) for c in (1, 0) if b or c]
FAR = [(a, 0, 0) for a in (2, 1, 3)]
DENSE = 3 * SLIDES + 2


def dense_row(name):
    return jnp.where(name >= HALF, name + (PADDED - HALF), name)


def place_of(a, b):
    at = (a + 1) * 3 + b + 1
    return at - (at > 4)


def slot_of(a, b, c):
    return (a * SIDE + b) * 2 + c


def kernel(
    nx, ny, emb, nbr, sid, live, cent, out, outc,
    embv, nbrv, sidv, centv, own, nb, cmat, zs, whi, wlo, cpad, e0, e2, e2t, n0, n1,
    f0, r0, f2, r2, f3, r3, s1, q1, s2, q2, s3, q3, s4, q4,
    load, halo_s, halo_r, ss, rs, seen,
):
    cells = own.shape[1] - 8 * BOUND
    dr = s2.shape[2]
    x, y = lax.axis_index("tx"), lax.axis_index("ty")
    core, chip = lax.rem(y, 2), y // 2
    chip_y, chip_x = chip // SIDE, lax.rem(chip, SIDE)
    pair = core * (SIDE * SIDE) + chip
    across = sorted(range(1, nx), key=lambda r: -min(r, nx - r))

    def on_tx(r):
        return (lax.rem(x + r, nx), y)

    def on_ty(a, b, c):
        to = lax.rem(chip_y + a, SIDE) * SIDE + lax.rem(chip_x + b, SIDE)
        return (x, to * 2 + lax.rem(core + c, 2))

    get_ids = pltpu.make_async_copy(nbr, nbrv, load.at[0])
    get_ids.start()
    get_emb = pltpu.make_async_copy(emb, embv, load.at[1])
    get_emb.start()
    get_sid = pltpu.make_async_copy(sid, sidv, load.at[2])
    get_sid.start()
    get_cent = pltpu.make_async_copy(cent, centv, load.at[3])
    get_cent.start()

    bar = pltpu.get_barrier_semaphore()

    def tile(a, b):
        return (lax.rem(x + a + nx, nx), lax.rem(y + b + ny, ny))

    def greet(sem, a, b):
        pl.semaphore_signal(sem, inc=1, device_id=tile(a, b), device_id_type=MESH)

    border = [(a, b) for a in (-1, 1) for b in (-1, 1)] + [(-1, 0), (1, 0), (0, -1), (0, 1)]
    other = 1 - 2 * core
    first_met = border + [(a, b) for a in (-4, -3, -2, 2, 3, 4) for b in (0, other)]
    for a, b in first_met:
        greet(bar, a, b)

    def greet_tx(step, d):
        for a in (-d, d):
            greet(seen.at[step], a, 0)

    def greet_ty(step, d):
        for b in (-d, d):
            greet(seen.at[step], 0, b)

    def heard(step):
        pl.semaphore_wait(seen.at[step], 2)

    r0[:, :, SLOTS:, :] = jnp.zeros((ITERS, 2 * nx, 8 - SLOTS, LANES), F32)
    r2[:, :, HALF:, :] = jnp.zeros((ITERS, SIDE * SIDE, PADDED - HALF, LANES), F32)
    r3[:, :, HALF:, :] = jnp.zeros((ITERS, 2, PADDED - HALF, LANES), F32)
    q1[:, :, SENT:, :] = jnp.zeros((ITERS, ny, CHUNK - SENT, LANES), F32)
    q4[:, PAIRS * BACK :, :] = jnp.zeros((ITERS, q4.shape[1] - PAIRS * BACK, LANES), F32)
    cpad[...] = jnp.zeros_like(cpad)
    own[PCS:, :cells] = jnp.zeros((ROWS - PCS, cells), F32)
    get_ids.wait()
    ids = nbrv[:, 0, 0, :]
    center = 5 * BOUND + cells - BOUND
    ids = jnp.where(ids < center, ids, jnp.where(ids < center + BOUND, ids - center, ids - BOUND))
    for n in range(ids.shape[0]):
        nb[n] = jnp.broadcast_to(ids[n : n + 1, :], (8, cells))
    rows8 = iota((8, cells), 0)

    def count(g, c):
        base = rows8 + g * 16
        low = jnp.zeros((8, cells), F32)
        high = jnp.zeros((8, cells), F32)
        for n in range(ids.shape[0]):
            here = nb[n]
            low = low + jnp.where(here == base, 1.0, 0.0)
            high = high + jnp.where(here == base + 8, 1.0, 0.0)
        at = pl.multiple_of(g * 16, 16)
        cmat[pl.ds(at, 16), :] = jnp.concatenate([low, high], axis=0).astype(BF16)
        return c

    groups = cmat.shape[0] // 16
    early = groups * 8 // 16
    lax.fori_loop(0, early, count, 0)
    get_emb.wait()
    own[:PCS, :cells] = embv[:, 0, 0, :]

    pl.semaphore_wait(bar, len(first_met))

    for a, b in border:
        pltpu.make_async_remote_copy(
            src_ref=own.at[:, pl.ds(0, BOUND)],
            dst_ref=own.at[:, pl.ds(cells + place_of(a, b) * BOUND, BOUND)],
            send_sem=halo_s,
            recv_sem=halo_r,
            device_id=tile(-a, -b),
            device_id_type=MESH,
        ).start()
    halo = pltpu.make_async_remote_copy(
        src_ref=own.at[:, pl.ds(cells, 8 * BOUND)],
        dst_ref=own.at[:, pl.ds(cells, 8 * BOUND)],
        send_sem=halo_s,
        recv_sem=halo_r,
        device_id=on_tx(1),
        device_id_type=MESH,
    )

    greet_tx(0, 4)
    greet_ty(1, 1)
    lax.fori_loop(early, groups, count, 0)

    alive = iota((1, cells), 1) < live[...]
    livef = alive.astype(F32)
    get_sid.wait()
    slides = sidv[0].astype(F32)
    left = jnp.where(alive, slides, 64.0)
    masks, names = [], []
    for _ in range(SLOTS):
        name = jnp.min(left, axis=1, keepdims=True)
        masks.append(jnp.where(left == name, livef, 0.0))
        names.append(jnp.where(name < 64.0, name, NONE))
        left = jnp.where(left > name, left, 64.0)
    row = iota((8, cells), 0)

    def stack(parts):
        total = jnp.zeros((8, cells), F32)
        for at, part in parts:
            total = total + jnp.where(row == at, part, 0.0)
        return total

    by_slot = list(enumerate(masks))
    mask8 = stack(by_slot)
    mask8_bf = mask8.astype(BF16)
    masked = stack(by_slot + [(SLOTS, 1.0 - livef)])
    masked2 = jnp.concatenate([masked, masked], axis=0).astype(BF16)
    slot_row = iota((8, LANES), 0)
    slot_lane = iota((8, LANES), 1)
    name8 = jnp.full((8, LANES), NONE, F32)
    for i in range(SLOTS):
        name8 = jnp.where(slot_row == i, dense_row(names[i]), name8)
    here8_bf = jnp.where(slot_lane.astype(F32) == name8, 1.0, 0.0)[:, : 2 * PADDED].astype(BF16)
    own_name8 = jnp.full((8, LANES), NONE, F32)
    for i in range(SLOTS):
        own_name8 = jnp.where(slot_row == i, names[i], own_name8)
    n0[...] = own_name8
    n1[0] = own_name8
    get_cent.wait()
    cpad[:PCS, :CLUSTERS] = centv[...]
    centre = cpad[...]

    heard(1)
    greet_ty(2, 2)
    halo.wait_recv()
    everything = own[...]
    part1 = everything.astype(BF16).astype(F32)
    rest = everything - part1
    part2 = rest.astype(BF16).astype(F32)
    parts = jnp.concatenate([part1, part2, rest - part2], axis=0).astype(BF16)
    summed = dot(parts, cmat[...], NN)
    summed = (summed[2 * ROWS :] + summed[ROWS : 2 * ROWS]) + summed[:ROWS]
    field = (everything[:, :cells] + summed) / (ids.shape[0] + 1.0)
    field = jnp.where(iota((ROWS, cells), 0) < PCS, field, 0.0) * livef

    heard(2)
    greet_ty(3, 4)
    heard(0)

    cluster = iota((LANES, cells), 0)
    lane40 = iota((1, LANES), 1)

    def sender(sem):
        def send(src, dst, to):
            pltpu.make_async_remote_copy(
                src_ref=src, dst_ref=dst, send_sem=ss.at[sem], recv_sem=rs.at[sem],
                device_id=to, device_id_type=MESH,
            ).start()

        return send

    def arrivals(sem, region):
        return pltpu.make_async_remote_copy(
            src_ref=region, dst_ref=region, send_sem=ss.at[sem], recv_sem=rs.at[sem],
            device_id=on_tx(1), device_id_type=MESH,
        )

    pending = []
    at_pairs = []
    for turn in range(ITERS):
        sem = turn * 8
        unit_y = centre * lax.rsqrt(jnp.sum(centre * centre, axis=0, keepdims=True) + 1.0)
        inverse = lax.rsqrt(jnp.sum(field * field, axis=0, keepdims=True) + 1.0)
        unit_z = field * inverse
        zs[...] = field
        yh, yl = parts_of(unit_y)
        zh, zl = parts_of(unit_z)
        score = dot(
            jnp.concatenate([yh, yh, yl, yl], axis=0).astype(BF16),
            jnp.concatenate([zh, zl, zh, zl], axis=0).astype(BF16),
            TN,
        )
        raw = jnp.where(cluster < CLUSTERS, jnp.exp(SHARPNESS * (score - 1.0)), 0.0)
        first = raw * (livef / jnp.sum(raw, axis=0, keepdims=True))
        first = jnp.where(cluster == LIVE_LANE, livef, first)
        occ = halves(dot(mask8_bf, jnp.concatenate(split2(first), axis=0), NT))
        occ = jnp.where(slot_lane == ID_LANE, name8, occ)

        f0[turn] = occ
        send = sender(sem)
        for r in across + [0]:
            for c in (1, 0):
                if r or c:
                    send(
                        f0.at[turn, pl.ds(0, SLOTS)],
                        r0.at[turn, r * 2 + c, pl.ds(0, SLOTS)],
                        (lax.rem(x + r, nx), chip * 2 + lax.rem(core + c, 2)),
                    )
        r0[turn, 0, :SLOTS] = occ[:SLOTS]

        if turn == 0:
            heard(3)
            greet_ty(4, 8)

        slots_a = stack(by_slot + [(4, inverse)] + [(5 + i, masks[i]) for i in range(3)])
        slots_b = stack([(0, masks[3]), (1, inverse)])
        ones_b = stack([(2 + i, masks[i]) for i in range(SLOTS)])

        def build(p, c):
            one = zs[pl.ds(p * 2, 1), :]
            two = zs[pl.ds(p * 2 + 1, 1), :]
            upper = jnp.where(row < 5, one, two) * slots_a
            lower = two * slots_b + ones_b
            hi, lo = split2(jnp.concatenate([upper, lower], axis=0))
            at = pl.multiple_of(p * CHUNK, CHUNK)
            whi[pl.ds(at, CHUNK), :] = hi
            wlo[pl.ds(at, CHUNK), :] = lo
            return c

        lax.fori_loop(0, PAIRS, build, 0)

        if turn == 0:
            heard(4)
            send = sender(7 * ITERS + ITERS)
            for offset in OTHERS:
                send(n0.at[pl.ds(0, SLOTS)], n1.at[slot_of(*offset), pl.ds(0, SLOTS)], on_ty(*offset))
        copy = arrivals(sem, r0.at[turn, pl.ds(1, 2 * nx - 1), pl.ds(0, SLOTS)])
        copy.wait_recv()
        pending.append(copy)
        got = r0[turn].reshape(2 * nx * 8, LANES)
        if turn == 0:
            name = jnp.broadcast_to(got[:, ID_LANE : ID_LANE + 1], got.shape)
            half_row = (iota(got.shape, 1) + core * PADDED).astype(F32)
            slot = lax.rem(iota(got.shape, 0), 8)
            e0[...] = jnp.where((name == half_row) & (slot < SLOTS), 1.0, 0.0).astype(BF16)
        part = halves(dot(e0[...], split_lanes(got), TN)[:PADDED])
        f2[turn] = part
        send = sender(sem + 2)
        for a, b in SQUARE[:-1]:
            send(
                f2.at[turn, pl.ds(0, HALF)],
                r2.at[turn, a * SIDE + b, pl.ds(0, HALF)],
                on_ty(a, b, 0),
            )
        r2[turn, 0] = part
        if turn == 0:
            told = arrivals(7 * ITERS + ITERS, n1.at[pl.ds(1, ny - 1), pl.ds(0, SLOTS)])
            told.wait_recv()
            pending.append(told)
            name4 = n1[:, :SLOTS, :]
            gap = jnp.zeros((ny, 1, LANES), F32)
            name = jnp.concatenate([name4, gap, name4, gap, name4, gap, gap], axis=1)
            shape = (ny * CHUNK, LANES)
            name = name.reshape(shape)
            at = lax.rem(iota(shape, 0), CHUNK)
            second = (at >= 5) & (at < 10)
            middle = (at == 4) | (at == 9)
            start = jnp.where(
                middle,
                3 * SLIDES + second.astype(jnp.int32),
                jnp.where(second, SLIDES, jnp.where(at >= 10, 2 * SLIDES, 0)),
            ).astype(F32)
            goal = start + jnp.where(middle, 0.0, jnp.where(at < SENT, name, NONE))
            table = jnp.where(goal == iota(shape, 1).astype(F32), 1.0, 0.0)
            e2[...] = table.astype(BF16)
            e2t[...] = table.T.astype(BF16)
        copy = arrivals(sem + 2, r2.at[turn, pl.ds(1, SIDE * SIDE - 1), pl.ds(0, HALF)])
        copy.wait_recv()
        pending.append(copy)
        part = jnp.sum(r2[turn], axis=0)
        f3[turn] = part
        send = sender(sem + 7)
        send(f3.at[turn, pl.ds(0, HALF)], r3.at[turn, core, pl.ds(0, HALF)], on_ty(0, 0, 1))
        r3[turn, core] = part
        copy = arrivals(sem + 7, r3.at[turn, 0, pl.ds(0, HALF)])
        copy.wait_recv()
        pending.append(copy)
        occupied = r3[turn].reshape(2 * PADDED, LANES)
        totals = occupied[:, LIVE_LANE : LIVE_LANE + 1]
        expected = (
            jnp.sum(occupied, axis=0, keepdims=True)
            * totals
            / jnp.sum(totals, axis=0, keepdims=True)
        )
        ratio = (expected + 1.0) / (occupied + 1.0)
        ratio = jnp.where(lane40 < CLUSTERS, ratio * ratio, 1.0)
        mine = dot(here8_bf, split_lanes(ratio), NN)
        mine_hi = jnp.where(slot_row == SLOTS, 1.0, mine[:, :LANES])
        mine2 = jnp.concatenate([mine_hi, mine[:, LANES:]], axis=0).astype(BF16)
        weighted = raw * dot(mine2, masked2, TN)
        assign = weighted * (livef / jnp.sum(weighted, axis=0, keepdims=True))

        ah, al = split2(assign)
        both = jnp.concatenate([ah, al], axis=0)
        send = sender(sem + 3)
        chips = SIDE * SIDE
        for side, count_ in ((0, chips), (1, PAIRS - chips)):
            rows = pl.ds(side * chips * CHUNK, count_ * CHUNK)
            wide = dot(whi[rows, :], both, NT)
            sums = halves(wide) + dot(wlo[rows, :], ah, NT)
            s1[turn, pl.ds(side * chips, count_)] = sums.reshape(count_, CHUNK, LANES)
            c = lax.rem(core + side, 2)
            for a, b in SQUARE:
                to = lax.rem(chip_y + a, SIDE) * SIDE + lax.rem(chip_x + b, SIDE)

                def go(a=a, b=b, to=to, c=c, side=side):
                    send(
                        s1.at[turn, side * chips + to, pl.ds(0, SENT)],
                        q1.at[turn, (a * SIDE + b) * 2 + c, pl.ds(0, SENT)],
                        (x, to * 2 + side),
                    )

                if side == 0 and (a or b):
                    go()
                elif side == 0:
                    pl.when(core != side)(go)
                elif a or b:
                    pl.when(to < count_)(go)
                else:
                    pl.when((core != side) & (to < count_))(go)

        @pl.when(pair < PAIRS)
        def _():
            q1[turn, 0, :SENT] = s1[turn, pair, :SENT]
            arrivals(sem + 3, q1.at[turn, pl.ds(1, ny - 1), pl.ds(0, SENT)]).wait_recv()
            got = q1[turn].reshape(ny * CHUNK, LANES)
            part = halves(dot(e2t[...], split_lanes(got), NN))
            s2[turn] = part.reshape(nx, dr, LANES)

            send = sender(sem + 4)
            for r in across:
                send(s2.at[turn, lax.rem(x + r, nx)], q2.at[turn, r], on_tx(r))
            q2[turn, 0] = s2[turn, x]
            arrivals(sem + 4, q2.at[turn, pl.ds(1, nx - 1)]).wait_recv()
            part = jnp.sum(q2[turn], axis=0)
            s3[turn] = part
            send = sender(sem + 5)
            for r in across:
                send(s3.at[turn], q3.at[turn, x], on_tx(r))
            q3[turn, x] = part
            arrivals(sem + 5, q3.at[turn, pl.ds(1, nx - 1)]).wait_recv()
            whole = q3[turn].reshape(nx * dr, LANES)
            counts = whole[2 * SLIDES : 3 * SLIDES]
            scale = 1.0 / (counts + 1.0)
            weight = jnp.sum(counts * scale, axis=0, keepdims=True)
            weight = jnp.where(lane40 < CLUSTERS, weight, 1.0)
            betas = []
            for j in range(2):
                part = whole[j * SLIDES : (j + 1) * SLIDES]
                mean = jnp.sum(part * scale, axis=0, keepdims=True) / weight
                betas.append((part - counts * mean) * scale)
            betas.append(whole[2 * SLIDES :])
            betas = split_lanes(jnp.concatenate(betas, axis=0))

            send = sender(sem + 6)
            group = 2 * SIDE
            for a in (2, 1, 3, 0):
                rows = pl.ds(a * group * CHUNK, group * CHUNK)
                chosen = halves(dot(e2[rows, :], betas, NN))
                s4[turn, pl.ds(a * group, group)] = chosen.reshape(group, CHUNK, LANES)
                for b in (2, 1, 3, 0):
                    for c in (1, 0):
                        if a or b or c:
                            send(
                                s4.at[turn, slot_of(a, b, c), pl.ds(0, BACK)],
                                q4.at[turn, pl.ds(pair * BACK, BACK)],
                                on_ty(SIDE - a, SIDE - b, 2 - c),
                            )
            q4[turn, pl.ds(pair * BACK, BACK)] = s4[turn, 0, :BACK]
            arrivals(sem + 6, q4.at[turn, pl.ds(0, (PAIRS - 1) * BACK)]).wait_recv()

        @pl.when(pair >= PAIRS)
        def _():
            arrivals(sem + 6, q4.at[turn, pl.ds(0, PAIRS * BACK)]).wait_recv()

        slot_beta = [q4[turn, pl.ds(i, ROWS, stride=5), :] for i in range(SLOTS)]
        bh, bl = split2(jnp.concatenate(slot_beta, axis=0))
        shifts = dot(jnp.concatenate([bh, bh], axis=1), both, NN) + dot(bl, ah, NN)
        for i in range(SLOTS):
            field = field - shifts[i * ROWS : (i + 1) * ROWS] * masks[i]
        centre = q4[turn, pl.ds(SLOTS, ROWS, stride=5), :]

    out[:, 0, 0, :] = field[:PCS]
    unit_y = centre / jnp.sqrt(jnp.sum(centre * centre, axis=0, keepdims=True) + 1.0)
    outc[...] = unit_y[:PCS, :CLUSTERS]

    halo.wait_send()
    for copy in pending:
        copy.wait_send()
    for turn in range(ITERS):
        sem = turn * 8

        @pl.when(pair < PAIRS)
        def _():
            arrivals(sem + 3, q1.at[turn, pl.ds(0, PAIRS - 1), pl.ds(0, SENT)]).wait_send()
            arrivals(sem + 4, q2.at[turn, pl.ds(1, nx - 1)]).wait_send()
            arrivals(sem + 5, q3.at[turn, pl.ds(1, nx - 1)]).wait_send()
            arrivals(sem + 6, s4.at[turn, pl.ds(1, ny - 1), pl.ds(0, BACK)]).wait_send()

        @pl.when(pair >= PAIRS)
        def _():
            arrivals(sem + 3, q1.at[turn, pl.ds(0, PAIRS), pl.ds(0, SENT)]).wait_send()


def hand_over(a, b, c, d, sems):
    copies = [
        pltpu.make_async_copy(a, c, sems.at[0]),
        pltpu.make_async_copy(b, d, sems.at[1]),
    ]
    for copy in copies:
        copy.start()
    for copy in copies:
        copy.wait()


def per_device(nx, ny, embedding, neighbors, slide_id, live_count, centroids):
    cells = embedding.shape[3]
    near = neighbors.shape[0]
    dr = -(-DENSE // (nx * 8)) * 8
    vmem = pl.BlockSpec(memory_space=pltpu.VMEM)
    hbm = pl.BlockSpec(memory_space=pltpu.HBM)

    def far(v):
        return pltpu.with_memory_space_constraint(v, pltpu.HBM)

    def buf(*shape):
        return pltpu.VMEM((ITERS,) + shape, F32)

    corrected, centers = pl.pallas_call(
        functools.partial(kernel, nx, ny),
        out_shape=(
            jax.ShapeDtypeStruct(embedding.shape, F32),
            jax.ShapeDtypeStruct((PCS, CLUSTERS), F32),
        ),
        in_specs=[hbm, hbm, hbm, vmem, hbm],
        out_specs=(vmem, vmem),
        scratch_shapes=[
            pltpu.VMEM(embedding.shape, F32),
            pltpu.VMEM(neighbors.shape, jnp.int32),
            pltpu.VMEM(slide_id.shape, jnp.int32),
            pltpu.VMEM((PCS, CLUSTERS), F32),
            pltpu.VMEM((ROWS, cells + 8 * BOUND), F32),
            pltpu.VMEM((near, 8, cells), jnp.int32),
            pltpu.VMEM((cells + 8 * BOUND, cells), BF16),
            pltpu.VMEM((ROWS, cells), F32),
            pltpu.VMEM((PAIRS * CHUNK, cells), BF16),
            pltpu.VMEM((PAIRS * CHUNK, cells), BF16),
            pltpu.VMEM((ROWS, LANES), F32),
            pltpu.VMEM((2 * nx * 8, LANES), BF16),
            pltpu.VMEM((ny * CHUNK, LANES), BF16),
            pltpu.VMEM((LANES, ny * CHUNK), BF16),
            pltpu.VMEM((8, LANES), F32),
            pltpu.VMEM((ny, 8, LANES), F32),
            buf(8, LANES),
            buf(2 * nx, 8, LANES),
            buf(PADDED, LANES),
            buf(SIDE * SIDE, PADDED, LANES),
            buf(PADDED, LANES),
            buf(2, PADDED, LANES),
            buf(PAIRS, CHUNK, LANES),
            buf(ny, CHUNK, LANES),
            buf(nx, dr, LANES),
            buf(nx, dr, LANES),
            buf(dr, LANES),
            buf(nx, dr, LANES),
            buf(ny, CHUNK, LANES),
            buf(ROWS * 5 + 8, LANES),
            pltpu.SemaphoreType.DMA((4,)),
            pltpu.SemaphoreType.DMA,
            pltpu.SemaphoreType.DMA,
            pltpu.SemaphoreType.DMA((8 * ITERS + 1,)),
            pltpu.SemaphoreType.DMA((8 * ITERS + 1,)),
            pltpu.SemaphoreType.REGULAR((5,)),
        ],
        compiler_params=pltpu.CompilerParams(
            collective_id=0, has_side_effects=True, vmem_limit_bytes=48 * 1024 * 1024
        ),
        name="harmony",
    )(far(embedding), far(neighbors), far(slide_id), live_count, far(centroids.T))
    corrected, centers = pl.pallas_call(
        hand_over,
        out_shape=(
            jax.ShapeDtypeStruct(embedding.shape, F32),
            jax.ShapeDtypeStruct((PCS, CLUSTERS), F32),
        ),
        in_specs=[vmem] * 2,
        out_specs=(hbm, hbm),
        scratch_shapes=[pltpu.SemaphoreType.DMA((2,))],
        name="handover",
    )(
        pltpu.with_memory_space_constraint(corrected, pltpu.VMEM),
        pltpu.with_memory_space_constraint(centers, pltpu.VMEM),
    )
    return corrected, centers.T


def solution(mesh):
    nx, ny = mesh.shape["tx"], mesh.shape["ty"]
    placed = (
        P(None, "tx", "ty", None),
        P(None, "tx", "ty", None),
        P("tx", "ty", None),
        P("tx", "ty"),
        P(),
    )
    return jax.shard_map(
        functools.partial(per_device, nx, ny),
        mesh=mesh,
        in_specs=placed,
        out_specs=(P(None, "tx", "ty", None), P()),
        check_vma=False,
    )
```

```python
import functools

import jax
import jax.numpy as jnp
from jax import lax
from jax.experimental import pallas as pl
from jax.experimental.pallas import tpu as pltpu
from jax.sharding import PartitionSpec as P

SLIDES = 40
SLOTS = 4
ITERS = 2
CLUSTERS = 100
PCS = 50
BOUND = 128
SHARPNESS = 20.0

LANES = 128
ROWS = 56
PAIRS = 25
CHUNK = 16
SENT = 14
BACK = 10
HALF = 20
PADDED = 24
ID_LANE = 126
LIVE_LANE = 127
NONE = -1000.0

F32 = jnp.float32
BF16 = jnp.bfloat16
MESH = pl.DeviceIdType.MESH

NN = (((1,), (0,)), ((), ()))
NT = (((1,), (1,)), ((), ()))
TN = (((0,), (0,)), ((), ()))


def dot(a, b, dims):
    return lax.dot_general(a, b, dims, preferred_element_type=F32)


def split2(v):
    hi = v.astype(BF16)
    return hi, (v - hi.astype(F32)).astype(BF16)


def halves(v):
    return v[:, :LANES] + v[:, LANES:]


def split_lanes(v):
    return jnp.concatenate(split2(v), axis=1)


def parts_of(v):
    hi = v.astype(BF16).astype(F32)
    return hi, v - hi


def iota(shape, dim):
    return lax.broadcasted_iota(jnp.int32, shape, dim)


SIDE = 4


def ring(a):
    return min(a, SIDE - a)


SQUARE = sorted(
    ((a, b) for a in range(SIDE) for b in range(SIDE)), key=lambda o: -ring(o[0]) - ring(o[1])
)
OTHERS = [(a, b, c) for a, b in SQUARE for c in (1, 0) if a or b or c]
NEAR = [(0, b, c) for b in (2, 1, 3, 0) for c in (1, 0) if b or c]
FAR = [(a, 0, 0) for a in (2, 1, 3)]
DENSE = 3 * SLIDES + 2


def dense_row(name):
    return jnp.where(name >= HALF, name + (PADDED - HALF), name)


def place_of(a, b):
    at = (a + 1) * 3 + b + 1
    return at - (at > 4)


def slot_of(a, b, c):
    return (a * SIDE + b) * 2 + c


def kernel(
    nx, ny, emb, nbr, sid, live, cent, out, outc,
    embv, nbrv, sidv, centv, own, nb, cmat, zs, whi, wlo, cpad, e0, e2, e2t, n0, n1,
    f0, r0, f2, r2, f3, r3, s1, q1, s2, q2, s3, q3, s4, q4,
    load, halo_s, halo_r, ss, rs, seen,
):
    cells = own.shape[1] - 8 * BOUND
    dr = s2.shape[2]
    x, y = lax.axis_index("tx"), lax.axis_index("ty")
    core, chip = lax.rem(y, 2), y // 2
    chip_y, chip_x = chip // SIDE, lax.rem(chip, SIDE)
    pair = core * (SIDE * SIDE) + chip
    across = sorted(range(1, nx), key=lambda r: -min(r, nx - r))

    def on_tx(r):
        return (lax.rem(x + r, nx), y)

    def on_ty(a, b, c):
        to = lax.rem(chip_y + a, SIDE) * SIDE + lax.rem(chip_x + b, SIDE)
        return (x, to * 2 + lax.rem(core + c, 2))

    get_ids = pltpu.make_async_copy(nbr, nbrv, load.at[0])
    get_ids.start()
    get_emb = pltpu.make_async_copy(emb, embv, load.at[1])
    get_emb.start()
    get_sid = pltpu.make_async_copy(sid, sidv, load.at[2])
    get_sid.start()
    get_cent = pltpu.make_async_copy(cent, centv, load.at[3])
    get_cent.start()

    bar = pltpu.get_barrier_semaphore()

    def tile(a, b):
        return (lax.rem(x + a + nx, nx), lax.rem(y + b + ny, ny))

    def greet(sem, a, b):
        pl.semaphore_signal(sem, inc=1, device_id=tile(a, b), device_id_type=MESH)

    border = [(a, b) for a in (-1, 1) for b in (-1, 1)] + [(-1, 0), (1, 0), (0, -1), (0, 1)]
    other = 1 - 2 * core
    first_met = border + [(a, b) for a in (-4, -3, -2, 2, 3, 4) for b in (0, other)]
    for a, b in first_met:
        greet(bar, a, b)

    def greet_tx(step, d):
        for a in (-d, d):
            greet(seen.at[step], a, 0)

    def greet_ty(step, d):
        for b in (-d, d):
            greet(seen.at[step], 0, b)

    def heard(step):
        pl.semaphore_wait(seen.at[step], 2)

    r0[:, :, SLOTS:, :] = jnp.zeros((ITERS, 2 * nx, 8 - SLOTS, LANES), F32)
    r2[:, :, HALF:, :] = jnp.zeros((ITERS, SIDE * SIDE, PADDED - HALF, LANES), F32)
    r3[:, :, HALF:, :] = jnp.zeros((ITERS, 2, PADDED - HALF, LANES), F32)
    q1[:, :, SENT:, :] = jnp.zeros((ITERS, ny, CHUNK - SENT, LANES), F32)
    q4[:, PAIRS * BACK :, :] = jnp.zeros((ITERS, q4.shape[1] - PAIRS * BACK, LANES), F32)
    cpad[...] = jnp.zeros_like(cpad)
    own[PCS:, :cells] = jnp.zeros((ROWS - PCS, cells), F32)
    get_ids.wait()
    ids = nbrv[:, 0, 0, :]
    center = 5 * BOUND + cells - BOUND
    ids = jnp.where(ids < center, ids, jnp.where(ids < center + BOUND, ids - center, ids - BOUND))
    for n in range(ids.shape[0]):
        nb[n] = jnp.broadcast_to(ids[n : n + 1, :], (8, cells))
    rows8 = iota((8, cells), 0)

    def count(g, c):
        base = rows8 + g * 16
        low = jnp.zeros((8, cells), F32)
        high = jnp.zeros((8, cells), F32)
        for n in range(ids.shape[0]):
            here = nb[n]
            low = low + jnp.where(here == base, 1.0, 0.0)
            high = high + jnp.where(here == base + 8, 1.0, 0.0)
        at = pl.multiple_of(g * 16, 16)
        cmat[pl.ds(at, 16), :] = jnp.concatenate([low, high], axis=0).astype(BF16)
        return c

    groups = cmat.shape[0] // 16
    early = groups * 8 // 16
    lax.fori_loop(0, early, count, 0)
    get_emb.wait()
    own[:PCS, :cells] = embv[:, 0, 0, :]

    pl.semaphore_wait(bar, len(first_met))

    for a, b in border:
        pltpu.make_async_remote_copy(
            src_ref=own.at[:, pl.ds(0, BOUND)],
            dst_ref=own.at[:, pl.ds(cells + place_of(a, b) * BOUND, BOUND)],
            send_sem=halo_s,
            recv_sem=halo_r,
            device_id=tile(-a, -b),
            device_id_type=MESH,
        ).start()
    halo = pltpu.make_async_remote_copy(
        src_ref=own.at[:, pl.ds(cells, 8 * BOUND)],
        dst_ref=own.at[:, pl.ds(cells, 8 * BOUND)],
        send_sem=halo_s,
        recv_sem=halo_r,
        device_id=on_tx(1),
        device_id_type=MESH,
    )

    greet_tx(0, 4)
    greet_ty(1, 1)
    lax.fori_loop(early, groups, count, 0)

    alive = iota((1, cells), 1) < live[...]
    livef = alive.astype(F32)
    get_sid.wait()
    slides = sidv[0].astype(F32)
    left = jnp.where(alive, slides, 64.0)
    masks, names = [], []
    for _ in range(SLOTS):
        name = jnp.min(left, axis=1, keepdims=True)
        masks.append(jnp.where(left == name, livef, 0.0))
        names.append(jnp.where(name < 64.0, name, NONE))
        left = jnp.where(left > name, left, 64.0)
    row = iota((8, cells), 0)

    def stack(parts):
        total = jnp.zeros((8, cells), F32)
        for at, part in parts:
            total = total + jnp.where(row == at, part, 0.0)
        return total

    by_slot = list(enumerate(masks))
    mask8 = stack(by_slot)
    mask8_bf = mask8.astype(BF16)
    masked = stack(by_slot + [(SLOTS, 1.0 - livef)])
    masked2 = jnp.concatenate([masked, masked], axis=0).astype(BF16)
    slot_row = iota((8, LANES), 0)
    slot_lane = iota((8, LANES), 1)
    name8 = jnp.full((8, LANES), NONE, F32)
    for i in range(SLOTS):
        name8 = jnp.where(slot_row == i, dense_row(names[i]), name8)
    here8_bf = jnp.where(slot_lane.astype(F32) == name8, 1.0, 0.0)[:, : 2 * PADDED].astype(BF16)
    own_name8 = jnp.full((8, LANES), NONE, F32)
    for i in range(SLOTS):
        own_name8 = jnp.where(slot_row == i, names[i], own_name8)
    n0[...] = own_name8
    n1[0] = own_name8
    get_cent.wait()
    cpad[:PCS, :CLUSTERS] = centv[...]
    centre = cpad[...]

    heard(1)
    greet_ty(2, 2)
    halo.wait_recv()
    everything = own[...]
    part1 = everything.astype(BF16).astype(F32)
    rest = everything - part1
    part2 = rest.astype(BF16).astype(F32)
    parts = jnp.concatenate([part1, part2, rest - part2], axis=0).astype(BF16)
    summed = dot(parts, cmat[...], NN)
    summed = (summed[2 * ROWS :] + summed[ROWS : 2 * ROWS]) + summed[:ROWS]
    field = (everything[:, :cells] + summed) / (ids.shape[0] + 1.0)
    field = jnp.where(iota((ROWS, cells), 0) < PCS, field, 0.0) * livef

    heard(0)

    cluster = iota((LANES, cells), 0)
    lane40 = iota((1, LANES), 1)

    def sender(sem):
        def send(src, dst, to):
            pltpu.make_async_remote_copy(
                src_ref=src, dst_ref=dst, send_sem=ss.at[sem], recv_sem=rs.at[sem],
                device_id=to, device_id_type=MESH,
            ).start()

        return send

    def arrivals(sem, region):
        return pltpu.make_async_remote_copy(
            src_ref=region, dst_ref=region, send_sem=ss.at[sem], recv_sem=rs.at[sem],
            device_id=on_tx(1), device_id_type=MESH,
        )

    pending = []
    at_pairs = []
    for turn in range(ITERS):
        sem = turn * 8
        unit_y = centre * lax.rsqrt(jnp.sum(centre * centre, axis=0, keepdims=True) + 1.0)
        inverse = lax.rsqrt(jnp.sum(field * field, axis=0, keepdims=True) + 1.0)
        unit_z = field * inverse
        zs[...] = field
        yh, yl = parts_of(unit_y)
        zh, zl = parts_of(unit_z)
        score = dot(
            jnp.concatenate([yh, yh, yl, yl], axis=0).astype(BF16),
            jnp.concatenate([zh, zl, zh, zl], axis=0).astype(BF16),
            TN,
        )
        raw = jnp.where(cluster < CLUSTERS, jnp.exp(SHARPNESS * (score - 1.0)), 0.0)
        first = raw * (livef / jnp.sum(raw, axis=0, keepdims=True))
        first = jnp.where(cluster == LIVE_LANE, livef, first)
        occ = halves(dot(mask8_bf, jnp.concatenate(split2(first), axis=0), NT))
        occ = jnp.where(slot_lane == ID_LANE, name8, occ)

        f0[turn] = occ
        send = sender(sem)
        for r in across + [0]:
            for c in (1, 0):
                if r or c:
                    send(
                        f0.at[turn, pl.ds(0, SLOTS)],
                        r0.at[turn, r * 2 + c, pl.ds(0, SLOTS)],
                        (lax.rem(x + r, nx), chip * 2 + lax.rem(core + c, 2)),
                    )
        r0[turn, 0, :SLOTS] = occ[:SLOTS]

        if turn == 0:
            heard(2)
            greet_ty(3, 4)
            heard(3)
            greet_ty(4, 8)

        slots_a = stack(by_slot + [(4, inverse)] + [(5 + i, masks[i]) for i in range(3)])
        slots_b = stack([(0, masks[3]), (1, inverse)])
        ones_b = stack([(2 + i, masks[i]) for i in range(SLOTS)])

        def build(p, c):
            one = zs[pl.ds(p * 2, 1), :]
            two = zs[pl.ds(p * 2 + 1, 1), :]
            upper = jnp.where(row < 5, one, two) * slots_a
            lower = two * slots_b + ones_b
            hi, lo = split2(jnp.concatenate([upper, lower], axis=0))
            at = pl.multiple_of(p * CHUNK, CHUNK)
            whi[pl.ds(at, CHUNK), :] = hi
            wlo[pl.ds(at, CHUNK), :] = lo
            return c

        lax.fori_loop(0, PAIRS, build, 0)

        if turn == 0:
            heard(4)
            send = sender(7 * ITERS + ITERS)
            for offset in OTHERS:
                send(n0.at[pl.ds(0, SLOTS)], n1.at[slot_of(*offset), pl.ds(0, SLOTS)], on_ty(*offset))
        copy = arrivals(sem, r0.at[turn, pl.ds(1, 2 * nx - 1), pl.ds(0, SLOTS)])
        copy.wait_recv()
        pending.append(copy)
        got = r0[turn].reshape(2 * nx * 8, LANES)
        if turn == 0:
            name = jnp.broadcast_to(got[:, ID_LANE : ID_LANE + 1], got.shape)
            half_row = (iota(got.shape, 1) + core * PADDED).astype(F32)
            slot = lax.rem(iota(got.shape, 0), 8)
            e0[...] = jnp.where((name == half_row) & (slot < SLOTS), 1.0, 0.0).astype(BF16)
        part = halves(dot(e0[...], split_lanes(got), TN)[:PADDED])
        f2[turn] = part
        send = sender(sem + 2)
        for a, b in SQUARE[:-1]:
            send(
                f2.at[turn, pl.ds(0, HALF)],
                r2.at[turn, a * SIDE + b, pl.ds(0, HALF)],
                on_ty(a, b, 0),
            )
        r2[turn, 0] = part
        if turn == 0:
            told = arrivals(7 * ITERS + ITERS, n1.at[pl.ds(1, ny - 1), pl.ds(0, SLOTS)])
            told.wait_recv()
            pending.append(told)
            name4 = n1[:, :SLOTS, :]
            gap = jnp.zeros((ny, 1, LANES), F32)
            name = jnp.concatenate([name4, gap, name4, gap, name4, gap, gap], axis=1)
            shape = (ny * CHUNK, LANES)
            name = name.reshape(shape)
            at = lax.rem(iota(shape, 0), CHUNK)
            second = (at >= 5) & (at < 10)
            middle = (at == 4) | (at == 9)
            start = jnp.where(
                middle,
                3 * SLIDES + second.astype(jnp.int32),
                jnp.where(second, SLIDES, jnp.where(at >= 10, 2 * SLIDES, 0)),
            ).astype(F32)
            goal = start + jnp.where(middle, 0.0, jnp.where(at < SENT, name, NONE))
            table = jnp.where(goal == iota(shape, 1).astype(F32), 1.0, 0.0)
            e2[...] = table.astype(BF16)
            e2t[...] = table.T.astype(BF16)
        copy = arrivals(sem + 2, r2.at[turn, pl.ds(1, SIDE * SIDE - 1), pl.ds(0, HALF)])
        copy.wait_recv()
        pending.append(copy)
        part = jnp.sum(r2[turn], axis=0)
        f3[turn] = part
        send = sender(sem + 7)
        send(f3.at[turn, pl.ds(0, HALF)], r3.at[turn, core, pl.ds(0, HALF)], on_ty(0, 0, 1))
        r3[turn, core] = part
        copy = arrivals(sem + 7, r3.at[turn, 0, pl.ds(0, HALF)])
        copy.wait_recv()
        pending.append(copy)
        occupied = r3[turn].reshape(2 * PADDED, LANES)
        totals = occupied[:, LIVE_LANE : LIVE_LANE + 1]
        expected = (
            jnp.sum(occupied, axis=0, keepdims=True)
            * totals
            / jnp.sum(totals, axis=0, keepdims=True)
        )
        ratio = (expected + 1.0) / (occupied + 1.0)
        ratio = jnp.where(lane40 < CLUSTERS, ratio * ratio, 1.0)
        mine = dot(here8_bf, split_lanes(ratio), NN)
        mine_hi = jnp.where(slot_row == SLOTS, 1.0, mine[:, :LANES])
        mine2 = jnp.concatenate([mine_hi, mine[:, LANES:]], axis=0).astype(BF16)
        weighted = raw * dot(mine2, masked2, TN)
        assign = weighted * (livef / jnp.sum(weighted, axis=0, keepdims=True))

        ah, al = split2(assign)
        both = jnp.concatenate([ah, al], axis=0)
        send = sender(sem + 3)
        chips = SIDE * SIDE
        for side, count_ in ((0, chips), (1, PAIRS - chips)):
            rows = pl.ds(side * chips * CHUNK, count_ * CHUNK)
            wide = dot(whi[rows, :], both, NT)
            sums = halves(wide) + dot(wlo[rows, :], ah, NT)
            s1[turn, pl.ds(side * chips, count_)] = sums.reshape(count_, CHUNK, LANES)
            c = lax.rem(core + side, 2)
            for a, b in SQUARE:
                to = lax.rem(chip_y + a, SIDE) * SIDE + lax.rem(chip_x + b, SIDE)

                def go(a=a, b=b, to=to, c=c, side=side):
                    send(
                        s1.at[turn, side * chips + to, pl.ds(0, SENT)],
                        q1.at[turn, (a * SIDE + b) * 2 + c, pl.ds(0, SENT)],
                        (x, to * 2 + side),
                    )

                if side == 0 and (a or b):
                    go()
                elif side == 0:
                    pl.when(core != side)(go)
                elif a or b:
                    pl.when(to < count_)(go)
                else:
                    pl.when((core != side) & (to < count_))(go)

        @pl.when(pair < PAIRS)
        def _():
            q1[turn, 0, :SENT] = s1[turn, pair, :SENT]
            arrivals(sem + 3, q1.at[turn, pl.ds(1, ny - 1), pl.ds(0, SENT)]).wait_recv()
            got = q1[turn].reshape(ny * CHUNK, LANES)
            part = halves(dot(e2t[...], split_lanes(got), NN))
            s2[turn] = part.reshape(nx, dr, LANES)

            send = sender(sem + 4)
            for r in across:
                send(s2.at[turn, lax.rem(x + r, nx)], q2.at[turn, r], on_tx(r))
            q2[turn, 0] = s2[turn, x]
            arrivals(sem + 4, q2.at[turn, pl.ds(1, nx - 1)]).wait_recv()
            part = jnp.sum(q2[turn], axis=0)
            s3[turn] = part
            send = sender(sem + 5)
            for r in across:
                send(s3.at[turn], q3.at[turn, x], on_tx(r))
            q3[turn, x] = part
            arrivals(sem + 5, q3.at[turn, pl.ds(1, nx - 1)]).wait_recv()
            whole = q3[turn].reshape(nx * dr, LANES)
            counts = whole[2 * SLIDES : 3 * SLIDES]
            scale = 1.0 / (counts + 1.0)
            weight = jnp.sum(counts * scale, axis=0, keepdims=True)
            weight = jnp.where(lane40 < CLUSTERS, weight, 1.0)
            betas = []
            for j in range(2):
                part = whole[j * SLIDES : (j + 1) * SLIDES]
                mean = jnp.sum(part * scale, axis=0, keepdims=True) / weight
                betas.append((part - counts * mean) * scale)
            betas.append(whole[2 * SLIDES :])
            betas = split_lanes(jnp.concatenate(betas, axis=0))

            send = sender(sem + 6)
            group = 2 * SIDE
            for a in (2, 1, 3, 0):
                rows = pl.ds(a * group * CHUNK, group * CHUNK)
                chosen = halves(dot(e2[rows, :], betas, NN))
                s4[turn, pl.ds(a * group, group)] = chosen.reshape(group, CHUNK, LANES)
                for b in (2, 1, 3, 0):
                    for c in (1, 0):
                        if a or b or c:
                            send(
                                s4.at[turn, slot_of(a, b, c), pl.ds(0, BACK)],
                                q4.at[turn, pl.ds(pair * BACK, BACK)],
                                on_ty(SIDE - a, SIDE - b, 2 - c),
                            )
            q4[turn, pl.ds(pair * BACK, BACK)] = s4[turn, 0, :BACK]
            arrivals(sem + 6, q4.at[turn, pl.ds(0, (PAIRS - 1) * BACK)]).wait_recv()

        @pl.when(pair >= PAIRS)
        def _():
            arrivals(sem + 6, q4.at[turn, pl.ds(0, PAIRS * BACK)]).wait_recv()

        slot_beta = [q4[turn, pl.ds(i, ROWS, stride=5), :] for i in range(SLOTS)]
        bh, bl = split2(jnp.concatenate(slot_beta, axis=0))
        shifts = dot(jnp.concatenate([bh, bh], axis=1), both, NN) + dot(bl, ah, NN)
        for i in range(SLOTS):
            field = field - shifts[i * ROWS : (i + 1) * ROWS] * masks[i]
        centre = q4[turn, pl.ds(SLOTS, ROWS, stride=5), :]

    out[:, 0, 0, :] = field[:PCS]
    unit_y = centre / jnp.sqrt(jnp.sum(centre * centre, axis=0, keepdims=True) + 1.0)
    outc[...] = unit_y[:PCS, :CLUSTERS]

    halo.wait_send()
    for copy in pending:
        copy.wait_send()
    for turn in range(ITERS):
        sem = turn * 8

        @pl.when(pair < PAIRS)
        def _():
            arrivals(sem + 3, q1.at[turn, pl.ds(0, PAIRS - 1), pl.ds(0, SENT)]).wait_send()
            arrivals(sem + 4, q2.at[turn, pl.ds(1, nx - 1)]).wait_send()
            arrivals(sem + 5, q3.at[turn, pl.ds(1, nx - 1)]).wait_send()
            arrivals(sem + 6, s4.at[turn, pl.ds(1, ny - 1), pl.ds(0, BACK)]).wait_send()

        @pl.when(pair >= PAIRS)
        def _():
            arrivals(sem + 3, q1.at[turn, pl.ds(0, PAIRS), pl.ds(0, SENT)]).wait_send()


def hand_over(a, b, c, d, sems):
    copies = [
        pltpu.make_async_copy(a, c, sems.at[0]),
        pltpu.make_async_copy(b, d, sems.at[1]),
    ]
    for copy in copies:
        copy.start()
    for copy in copies:
        copy.wait()


def per_device(nx, ny, embedding, neighbors, slide_id, live_count, centroids):
    cells = embedding.shape[3]
    near = neighbors.shape[0]
    dr = -(-DENSE // (nx * 8)) * 8
    vmem = pl.BlockSpec(memory_space=pltpu.VMEM)
    hbm = pl.BlockSpec(memory_space=pltpu.HBM)

    def far(v):
        return pltpu.with_memory_space_constraint(v, pltpu.HBM)

    def buf(*shape):
        return pltpu.VMEM((ITERS,) + shape, F32)

    corrected, centers = pl.pallas_call(
        functools.partial(kernel, nx, ny),
        out_shape=(
            jax.ShapeDtypeStruct(embedding.shape, F32),
            jax.ShapeDtypeStruct((PCS, CLUSTERS), F32),
        ),
        in_specs=[hbm, hbm, hbm, vmem, hbm],
        out_specs=(vmem, vmem),
        scratch_shapes=[
            pltpu.VMEM(embedding.shape, F32),
            pltpu.VMEM(neighbors.shape, jnp.int32),
            pltpu.VMEM(slide_id.shape, jnp.int32),
            pltpu.VMEM((PCS, CLUSTERS), F32),
            pltpu.VMEM((ROWS, cells + 8 * BOUND), F32),
            pltpu.VMEM((near, 8, cells), jnp.int32),
            pltpu.VMEM((cells + 8 * BOUND, cells), BF16),
            pltpu.VMEM((ROWS, cells), F32),
            pltpu.VMEM((PAIRS * CHUNK, cells), BF16),
            pltpu.VMEM((PAIRS * CHUNK, cells), BF16),
            pltpu.VMEM((ROWS, LANES), F32),
            pltpu.VMEM((2 * nx * 8, LANES), BF16),
            pltpu.VMEM((ny * CHUNK, LANES), BF16),
            pltpu.VMEM((LANES, ny * CHUNK), BF16),
            pltpu.VMEM((8, LANES), F32),
            pltpu.VMEM((ny, 8, LANES), F32),
            buf(8, LANES),
            buf(2 * nx, 8, LANES),
            buf(PADDED, LANES),
            buf(SIDE * SIDE, PADDED, LANES),
            buf(PADDED, LANES),
            buf(2, PADDED, LANES),
            buf(PAIRS, CHUNK, LANES),
            buf(ny, CHUNK, LANES),
            buf(nx, dr, LANES),
            buf(nx, dr, LANES),
            buf(dr, LANES),
            buf(nx, dr, LANES),
            buf(ny, CHUNK, LANES),
            buf(ROWS * 5 + 8, LANES),
            pltpu.SemaphoreType.DMA((4,)),
            pltpu.SemaphoreType.DMA,
            pltpu.SemaphoreType.DMA,
            pltpu.SemaphoreType.DMA((8 * ITERS + 1,)),
            pltpu.SemaphoreType.DMA((8 * ITERS + 1,)),
            pltpu.SemaphoreType.REGULAR((5,)),
        ],
        compiler_params=pltpu.CompilerParams(
            collective_id=0, has_side_effects=True, vmem_limit_bytes=48 * 1024 * 1024
        ),
        name="harmony",
    )(far(embedding), far(neighbors), far(slide_id), live_count, far(centroids.T))
    corrected, centers = pl.pallas_call(
        hand_over,
        out_shape=(
            jax.ShapeDtypeStruct(embedding.shape, F32),
            jax.ShapeDtypeStruct((PCS, CLUSTERS), F32),
        ),
        in_specs=[vmem] * 2,
        out_specs=(hbm, hbm),
        scratch_shapes=[pltpu.SemaphoreType.DMA((2,))],
        name="handover",
    )(
        pltpu.with_memory_space_constraint(corrected, pltpu.VMEM),
        pltpu.with_memory_space_constraint(centers, pltpu.VMEM),
    )
    return corrected, centers.T


def solution(mesh):
    nx, ny = mesh.shape["tx"], mesh.shape["ty"]
    placed = (
        P(None, "tx", "ty", None),
        P(None, "tx", "ty", None),
        P("tx", "ty", None),
        P("tx", "ty"),
        P(),
    )
    return jax.shard_map(
        functools.partial(per_device, nx, ny),
        mesh=mesh,
        in_specs=placed,
        out_specs=(P(None, "tx", "ty", None), P()),
        check_vma=False,
    )
```
